128 devices in a mesh: leaf: 32 (over x, y, core), front: 4 (over z).
Axes of the slice: x: 4, y: 4, z: 4, core: 2. Of those that a mesh axis runs over, the one named last changes fastest.
Arguments:
- load_leaf: float32 [128, 196608], P(None, ('leaf', 'front')), may hold values from -6 to 6
- leaf_inverse: float32 [1536, 128, 128], P(('leaf', 'front')), may hold values from -1 to 1
- leaf_coupling: float32 [1536, 8, 128, 128], P(('leaf', 'front')), may hold values from -0.0625 to 0.0625
- leaf_pattern: int32 [1536, 8], P(('leaf', 'front')), may hold values from 0 to 61, all different within a row
- load_sep: float32 [128, 20480], P('front', 'leaf'), may hold values from -6 to 6
- sep_inverse: float32 [160, 128, 128], P('leaf'), may hold values from -1 to 1
- sep_coupling: float32 [6272, 128, 128], P('leaf'), may hold values from -0.09375 to 0.09375
Outputs:
- solution_leaf: float32 [128, 196608], P(None, ('leaf', 'front'))
- solution_sep: float32 [128, 20480], P('front', 'leaf')
The draws below stay inside these ranges and needn't reach their ends.
Inputs may be any that keep to these rules, and one draw needn't show every extreme that they name: `leaf_pattern`: the 8 entries of a row are different ancestor indices; every index 0 to 61 occurs in some row.
All inputs are finite; a program needn't handle non-finite values.
Results may differ from the reference program's by a relative error of at most 0.00011.
Values sent between devices are 32-bit elements; how exact they have to be, the bound alone decides.
No kernel may reach another device: no remote copies, remote signals or barrier semaphores. Data moves between devices by JAX's collectives and lax.ppermute only.
A program may use at most 128 MiB of HBM per device.

```python
import jax
import jax.numpy as jnp
from jax import lax

BLK = 128
R = 128
LBD = 12
KB = 8
LEVELS = 5
ANCB = 62
SEPBLK = 196
LEAFB = 1536
LEAF_ROWS = 196608
SEP_TOTAL = 20480
N_LEAF = 32
N_FRONT = 4


def draw_leaf_inverse(key, part):
    key = jax.random.fold_in(key, 11)
    key_diagonal, key_rest = jax.random.split(key)
    diagonal = jax.random.uniform(key_diagonal, (LEAFB, BLK), minval=0.5, maxval=1.0)
    off_diagonal = jnp.clip(jax.random.normal(key_rest, (LEAFB, BLK, BLK)), -4.0, 4.0) * (0.45 / BLK ** 0.5)
    identity = jnp.eye(BLK, dtype=jnp.float32)
    return off_diagonal * (1.0 - identity) + identity * diagonal[:, :, None]


def draw_sep_inverse(key, part):
    key = jax.random.fold_in(key, 23)
    key_diagonal, key_rest = jax.random.split(key)
    count_blocks = N_LEAF * LEVELS
    diagonal = jax.random.uniform(key_diagonal, (count_blocks, BLK), minval=0.5, maxval=1.0)
    off_diagonal = jnp.clip(jax.random.normal(key_rest, (count_blocks, BLK, BLK)), -4.0, 4.0) * (0.45 / BLK ** 0.5)
    identity = jnp.eye(BLK, dtype=jnp.float32)
    return off_diagonal * (1.0 - identity) + identity * diagonal[:, :, None]


def block_scale(rng, dims, shards, least, largest):
    def one(dim, blocks):
        steps = jax.random.uniform(jax.random.fold_in(jax.random.fold_in(rng, 6), dim), (blocks,), jnp.float32, least / len(shards), largest / len(shards))
        return jnp.repeat(jnp.exp(steps), dims[dim] // blocks).reshape((-1,) + (1,) * (len(dims) - dim - 1))

    loudness = one(*shards[0])
    for cut in shards[1:]:
        loudness = loudness * one(*cut)
    return loudness


def picks_of(stream_key, rows, number_of, top, lift):
    order = jax.random.permutation(jax.random.fold_in(stream_key, 1), number_of)
    favour = order
    for power in range(3):
        favour = favour * favour // number_of
    favour = favour * lift // number_of
    chance = jax.random.randint(jax.random.fold_in(stream_key, 2), (rows, number_of), 0, 4096) + favour
    holders = jax.random.permutation(jax.random.fold_in(stream_key, 3), rows)[jnp.arange(number_of) % rows]
    chance = jnp.where(jnp.arange(rows)[:, None] == holders[None, :], 1 << 14, chance)
    priority = chance * number_of + jnp.arange(number_of)
    return lax.top_k(priority.astype(jnp.int32), top)[1].astype(jnp.int32)


def scatter_about(key, extent, scale, most, shards=(), kind=jnp.bfloat16):
    gain = block_scale(key, extent, shards, -0.22, 0.18) if shards else 1.0
    entries = jax.random.normal(key, extent, jnp.float32) * scale * gain
    return jnp.minimum(jnp.maximum(entries, -most), most).astype(kind)


def setup_inputs(seed: int = 0) -> dict:
    seeds = jax.random.split(jax.random.key(seed), 8)
    return {
        "load_leaf": scatter_about(seeds[0], (R, LEAF_ROWS), 1.0, 6.0, ((1, 128),), jnp.float32),
        "leaf_inverse": draw_leaf_inverse(jax.random.fold_in(seeds[7], 71), 0),
        "leaf_coupling": scatter_about(seeds[2], (LEAFB, KB, BLK, BLK), (BLK * 64) ** -0.5, 0.0625, ((0, 128),), jnp.float32),
        "leaf_pattern": picks_of(seeds[3], LEAFB, ANCB, KB, 0),
        "load_sep": scatter_about(seeds[4], (R, SEP_TOTAL), 1.0, 6.0, ((0, 4), (1, 32)), jnp.float32),
        "sep_inverse": draw_sep_inverse(jax.random.fold_in(seeds[7], 71), 0),
        "sep_coupling": scatter_about(seeds[6], (N_LEAF * SEPBLK, BLK, BLK), (BLK * N_LEAF) ** -0.5, 0.09375, ((0, 32),), jnp.float32),
    }


def offsets_table(level_count):
    table_map = {}
    position = 0
    for upper_level in range(2, level_count + 1):
        for lower_level in range(1, upper_level):
            table_map[(upper_level, lower_level)] = position
            position = position + 2 ** upper_level
    return table_map


def reference(load_leaf, leaf_inverse, leaf_coupling, leaf_pattern, load_sep, sep_inverse, sep_coupling):
    highest = lax.Precision.HIGHEST
    per_leaf = N_FRONT * LBD
    leaf_rhs = load_leaf.reshape(R, N_LEAF, per_leaf, BLK)
    leaf_inv = leaf_inverse.reshape(N_LEAF, per_leaf, BLK, BLK)
    leaf_coup = leaf_coupling.reshape(N_LEAF, per_leaf, KB, BLK, BLK)
    leaf_patt = leaf_pattern.reshape(N_LEAF, per_leaf, KB)
    leaf_solved = jnp.einsum("rsbi,sbji->rsbj", leaf_rhs, leaf_inv, precision=highest)
    leaf_moved = jnp.moveaxis(leaf_solved, 1, 0)

    def leaf_terms(operands):
        solved_here, coupling_here, pattern_here = operands
        products = jnp.einsum("rbi,bqoi->bqro", solved_here, coupling_here, precision=highest)
        products = products.reshape(per_leaf * KB, R, BLK)
        return jax.ops.segment_sum(products, pattern_here.reshape(-1), num_segments=ANCB)

    ancestor_terms = lax.map(leaf_terms, (leaf_moved, leaf_coup, leaf_patt))
    sep_rhs = load_sep.reshape(R, N_LEAF, LEVELS, BLK)
    sep_inv = sep_inverse.reshape(N_LEAF, LEVELS, BLK, BLK)
    sep_coup = sep_coupling.reshape(N_LEAF, SEPBLK, BLK, BLK)
    table_map = offsets_table(LEVELS)
    sep_solved = []
    for upper_level in range(1, LEVELS + 1):
        span_blocks = 2 ** upper_level
        groups = N_LEAF // span_blocks
        portion = ancestor_terms[:, span_blocks - 2:2 * span_blocks - 2]
        portion = portion.reshape(groups, span_blocks, span_blocks, R, BLK).sum(axis=1)
        summed = jnp.moveaxis(portion.reshape(N_LEAF, R, BLK), 1, 0)
        for lower_level in range(1, upper_level):
            position = table_map[(upper_level, lower_level)]
            blocks = sep_coup[:, position:position + span_blocks].reshape(groups, span_blocks, span_blocks, BLK, BLK)
            lower_values = sep_solved[lower_level - 1].reshape(R, groups, span_blocks, BLK)
            summed = summed + jnp.einsum("rgmi,gdmoi->rgdo", lower_values, blocks, precision=highest).reshape(R, N_LEAF, BLK)
        residual = sep_rhs[:, :, upper_level - 1] - summed
        sep_solved.append(jnp.einsum("rdi,dji->rdj", residual, sep_inv[:, upper_level - 1], precision=highest))
    sep_final = [None] * LEVELS
    for upper_level in range(LEVELS, 0, -1):
        summed = jnp.zeros((R, N_LEAF, BLK), jnp.float32)
        for higher_level in range(upper_level + 1, LEVELS + 1):
            span_blocks = 2 ** higher_level
            groups = N_LEAF // span_blocks
            position = table_map[(higher_level, upper_level)]
            blocks = sep_coup[:, position:position + span_blocks].reshape(groups, span_blocks, span_blocks, BLK, BLK)
            higher_values = sep_final[higher_level - 1].reshape(R, groups, span_blocks, BLK)
            summed = summed + jnp.einsum("rgdo,gdmoi->rgmi", higher_values, blocks, precision=highest).reshape(R, N_LEAF, BLK)
        residual = sep_solved[upper_level - 1] - summed
        sep_final[upper_level - 1] = jnp.einsum("rdo,doi->rdi", residual, sep_inv[:, upper_level - 1], precision=highest)
    solution_sep = jnp.stack(sep_final, axis=2).reshape(R, N_LEAF * LEVELS * BLK)
    ancestor_parts = []
    for upper_level in range(1, LEVELS + 1):
        span_blocks = 2 ** upper_level
        groups = N_LEAF // span_blocks
        level_values = sep_final[upper_level - 1].reshape(R, groups, 1, span_blocks, BLK)
        level_values = jnp.broadcast_to(level_values, (R, groups, span_blocks, span_blocks, BLK))
        ancestor_parts.append(level_values.reshape(R, N_LEAF, span_blocks, BLK))
    ancestors = jnp.moveaxis(jnp.concatenate(ancestor_parts, axis=2), 1, 0)

    def leaf_back(operands):
        solved_here, coupling_here, pattern_here, ancestor_here, inverse_here = operands
        picked = ancestor_here[:, pattern_here]
        carried = jnp.einsum("rbqo,bqoi->rbi", picked, coupling_here, precision=highest)
        return jnp.einsum("rbo,boi->rbi", solved_here - carried, inverse_here, precision=highest)

    leaf_final = lax.map(leaf_back, (leaf_moved, leaf_coup, leaf_patt, ancestors, leaf_inv))
    solution_leaf = jnp.moveaxis(leaf_final, 0, 1).reshape(R, N_LEAF * per_leaf * BLK)
    return solution_leaf, solution_sep
```

```python
import jax
import jax.numpy as jnp
from jax import lax
from jax.sharding import PartitionSpec as P


def from_partner_2(shard, axis, bit):
    return lax.ppermute(shard, axis, [(i, i ^ 1 << bit) for i in range(lax.axis_size(axis))])


def offsets_table(level_count):
    table_map = {}
    position = 0
    for upper_level in range(2, level_count + 1):
        for lower_level in range(1, upper_level):
            table_map[upper_level, lower_level] = position
            position = position + 2**upper_level
    return table_map


def from_partner(values, bit_index):
    return from_partner_2(values, "leaf", bit_index)


def sum_to_owner(parts, axis):
    return lax.all_to_all(parts, axis, 0, 0).sum(axis=0)


def copies_of_all(shard, axis):
    copies = jnp.broadcast_to(shard, (lax.axis_size(axis),) + shard.shape)
    return lax.all_to_all(copies, axis, 0, 0)


def halve_blocks(buffer, leaf_id, level_count, block_size):
    columns = buffer.shape[0]
    portions = []
    for level_index in range(1, level_count + 1):
        first_row = (2**level_index - 2) * block_size
        last_row = (2 ** (level_index + 1) - 2) * block_size
        portions.append(buffer[:, first_row:last_row].reshape(columns, 2**level_index, block_size))
    for bit_index in range(level_count):
        my_bit = leaf_id >> bit_index & 1
        kept = []
        outgoing = []
        for level_index in range(bit_index + 1, level_count + 1):
            current = portions[level_index - 1]
            paired = current.reshape(columns, current.shape[1] // 2, 2, block_size)
            even_blocks = paired[:, :, 0]
            odd_blocks = paired[:, :, 1]
            kept.append(jnp.where(my_bit == 1, odd_blocks, even_blocks))
            outgoing.append(jnp.where(my_bit == 1, even_blocks, odd_blocks))
        incoming = from_partner(jnp.concatenate(outgoing, axis=1), bit_index)
        position = 0
        for offset_index, level_index in enumerate(range(bit_index + 1, level_count + 1)):
            count_blocks = kept[offset_index].shape[1]
            portions[level_index - 1] = (
                kept[offset_index] + incoming[:, position : position + count_blocks]
            )
            position = position + count_blocks
    return jnp.concatenate(portions, axis=1)


def expand_blocks(portions, leaf_id, bit_index):
    my_bit = leaf_id >> bit_index & 1
    active = portions[bit_index:]
    incoming = from_partner(jnp.concatenate(active, axis=1), bit_index)
    widened = []
    position = 0
    for current in active:
        count_blocks = current.shape[1]
        theirs = incoming[:, position : position + count_blocks]
        position = position + count_blocks
        lower_first = jnp.stack([current, theirs], axis=2)
        upper_first = jnp.stack([theirs, current], axis=2)
        merged = jnp.where(my_bit == 0, lower_first, upper_first)
        widened.append(merged.reshape(current.shape[0], 2 * count_blocks, current.shape[2]))
    return portions[:bit_index] + widened


def local(
    load_leaf, leaf_inverse, leaf_coupling, leaf_pattern, load_sep, sep_inverse, sep_coupling
):
    highest = lax.Precision.HIGH
    all_columns = load_leaf.shape[0]
    leaf_blocks = leaf_pattern.shape[0]
    block_size = leaf_inverse.shape[-1]
    leaf_count = lax.axis_size("leaf")
    level_count = leaf_count.bit_length() - 1
    ancestor_blocks = 2 ** (level_count + 1) - 2
    columns = load_sep.shape[0]
    leaf_id = lax.axis_index("leaf")
    table_map = offsets_table(level_count)
    leaf_solved = jnp.einsum(
        "rbi,bji->rbj",
        load_leaf.reshape(all_columns, leaf_blocks, block_size),
        leaf_inverse,
        precision=highest,
    )
    selector = (
        leaf_pattern[:, :, None] == jnp.arange(ancestor_blocks, dtype=jnp.int32)[None, None, :]
    ).astype(jnp.float32)
    products = jnp.einsum("rbi,bqoi->rbqo", leaf_solved, leaf_coupling, precision=highest)
    gathered_terms = jnp.einsum("rbqo,bqa->rao", products, selector, precision=highest)
    reduced = sum_to_owner(
        gathered_terms.reshape(lax.axis_size("front"), columns, ancestor_blocks * block_size),
        "front",
    )
    level_updates = halve_blocks(reduced, leaf_id, level_count, block_size)
    sep_rhs = load_sep.reshape(columns, level_count, block_size)
    gathered = []
    own_solved = []
    for upper_level in range(1, level_count + 1):
        span_blocks = 2**upper_level
        group_start = (leaf_id >> upper_level) * span_blocks
        summed = level_updates[:, upper_level - 1]
        for lower_level in range(1, upper_level):
            position = table_map[upper_level, lower_level]
            group_rows = lax.dynamic_slice_in_dim(
                gathered[lower_level - 1], group_start, span_blocks, 1
            )
            summed = summed + jnp.einsum(
                "rmi,moi->ro",
                group_rows,
                sep_coupling[position : position + span_blocks],
                precision=highest,
            )
        solved = jnp.einsum(
            "ri,ji->rj",
            sep_rhs[:, upper_level - 1] - summed,
            sep_inverse[upper_level - 1],
            precision=highest,
        )
        own_solved.append(solved)
        if upper_level < level_count:
            gathered.append(
                jnp.moveaxis(copies_of_all(solved, "leaf"), 0, 1)
            )
    own_final = [None] * level_count
    portions = [None] * level_count
    for upper_level in range(level_count, 0, -1):
        residual = own_solved[upper_level - 1]
        if upper_level < level_count:
            buffer = jnp.zeros((columns, leaf_count, block_size), jnp.float32)
            for higher_level in range(upper_level + 1, level_count + 1):
                span_blocks = 2**higher_level
                group_start = (leaf_id >> higher_level) * span_blocks
                position = table_map[higher_level, upper_level]
                spread = jnp.einsum(
                    "ro,moi->rmi",
                    own_final[higher_level - 1],
                    sep_coupling[position : position + span_blocks],
                    precision=highest,
                )
                existing = lax.dynamic_slice_in_dim(buffer, group_start, span_blocks, 1)
                buffer = lax.dynamic_update_slice_in_dim(buffer, existing + spread, group_start, 1)
            residual = residual - sum_to_owner(jnp.moveaxis(buffer, 1, 0), "leaf")
        final = jnp.einsum("ro,oi->ri", residual, sep_inverse[upper_level - 1], precision=highest)
        own_final[upper_level - 1] = final
        portions[upper_level - 1] = final[:, None, :]
        portions = expand_blocks(portions, leaf_id, upper_level - 1)
    solution_sep = jnp.stack(own_final, axis=1).reshape(columns, level_count * block_size)
    ancestors = jnp.concatenate(portions, axis=1).reshape(columns, ancestor_blocks * block_size)
    ancestors = copies_of_all(ancestors, "front").reshape(
        all_columns, ancestor_blocks, block_size
    )
    picked = jnp.einsum("rao,bqa->rbqo", ancestors, selector, precision=highest)
    carried = jnp.einsum("rbqo,bqoi->rbi", picked, leaf_coupling, precision=highest)
    solution_leaf = jnp.einsum(
        "rbo,boi->rbi", leaf_solved - carried, leaf_inverse, precision=highest
    )
    return (solution_leaf.reshape(all_columns, leaf_blocks * block_size), solution_sep)


def solution(mesh):
    return jax.shard_map(
        local,
        mesh=mesh,
        in_specs=(
            P(None, ("leaf", "front")),
            P(("leaf", "front"), None, None),
            P(("leaf", "front"), None, None, None),
            P(("leaf", "front"), None),
            P("front", "leaf"),
            P("leaf", None, None),
            P("leaf", None, None),
        ),
        out_specs=(P(None, ("leaf", "front")), P("front", "leaf")),
        check_vma=False,
    )
```

```python
import jax
import jax.numpy as jnp
from jax import lax
from jax.experimental import pallas as pl
from jax.experimental.pallas import tpu as pltpu
from jax.sharding import PartitionSpec as P

F32 = jnp.float32
BF16 = jnp.bfloat16
BLK = 128
COLS = 32
VMEM_BYTES = 48 * 1024 * 1024
RUNS = {(2, 1): 0, (3, 1): 4, (3, 2): 12, (4, 1): 20, (4, 2): 36, (4, 3): 52}
RUNS |= {(5, 1): 68, (5, 2): 100, (5, 3): 132, (5, 4): 164}
CHUNK = 8


def split(value):
    high = value.astype(BF16)
    low = (value - high.astype(F32)).astype(BF16)
    return high, low


def stacked(value):
    return jnp.concatenate(split(value), axis=0)


def beside(value):
    return jnp.concatenate(split(value), axis=1)


def dot_nt(left, right):
    return lax.dot_general(left, right, (((1,), (1,)), ((), ())), preferred_element_type=F32)


def dot_nn(left, right):
    return lax.dot_general(left, right, (((1,), (0,)), ((), ())), preferred_element_type=F32)


def fold(terms):
    rows = terms.shape[0] // 2
    return (terms[:rows, :BLK] + terms[:rows, BLK:]) + (terms[rows:, :BLK] + terms[rows:, BLK:])


def times_transposed(value, matrix):
    return fold(dot_nt(stacked(value), stacked(matrix)))


def times(value, matrix):
    return fold(dot_nn(stacked(value), beside(matrix)))


def sum_times_transposed(lefts, matrices):
    total = None
    for k in range(0, len(lefts), 2):
        left = jnp.concatenate([lefts[k], lefts[k + 1]], axis=1)
        right = jnp.concatenate([stacked(matrices[k]), stacked(matrices[k + 1])], axis=1)
        part = dot_nt(left, right)
        total = part if total is None else total + part
    return total


def wide_left(value):
    both = stacked(value)
    return jnp.concatenate([both, both], axis=1)


def two_times(left, first, second):
    right = jnp.concatenate([stacked(first), stacked(second)], axis=1)
    out = dot_nn(left, right)
    rows = out.shape[0] // 2
    out = out[:rows] + out[rows:]
    return out[:, :BLK], out[:, BLK:]


def call(body, name, coords, inputs, outs, in_any=(), scratch=(), flops=0):
    specs = [
        pl.BlockSpec(memory_space=pl.ANY if k in in_any else pltpu.VMEM)
        for k in range(len(inputs))
    ]
    return pl.pallas_call(
        body,
        name=name,
        out_shape=[jax.ShapeDtypeStruct(shape, F32) for shape in outs],
        grid_spec=pltpu.PrefetchScalarGridSpec(
            num_scalar_prefetch=1,
            grid=(1,),
            in_specs=specs,
            out_specs=[pl.BlockSpec(memory_space=pltpu.VMEM) for _ in outs],
            scratch_shapes=list(scratch),
        ),
        compiler_params=pltpu.CompilerParams(vmem_limit_bytes=VMEM_BYTES),
        cost_estimate=pl.CostEstimate(flops=flops, bytes_accessed=1 << 20, transcendentals=0),
    )(coords, *inputs)


def fetch(source, first, count, target, sems):
    for k in range(0, count, CHUNK):
        size = min(CHUNK, count - k)
        pltpu.make_async_copy(
            source.at[pl.ds(first + k, size)], target.at[pl.ds(k, size)], sems.at[k // CHUNK]
        ).start()


def fetched(source, first, count, target, sems):
    for k in range(0, count, CHUNK):
        size = min(CHUNK, count - k)
        pltpu.make_async_copy(
            source.at[pl.ds(first + k, size)], target.at[pl.ds(k, size)], sems.at[k // CHUNK]
        ).wait()


def matrices(count):
    return [pltpu.VMEM((count, BLK, BLK), F32), pltpu.SemaphoreType.DMA((-(-count // CHUNK),))]


def leaf_forward_kernel(
    coords, pattern, load, inverse, coupling, load_sep, solved, mine13, theirs13, mine45, theirs45, sums
):
    block = pl.program_id(0)
    core, y_at, x_at, front = coords[0], coords[1], coords[2], coords[3]

    @pl.when(block == 0)
    def _():
        sums[...] = jnp.zeros_like(sums)
        rows = pl.ds(pl.multiple_of(front * COLS, COLS), COLS)
        slots = (
            core,
            2 + (y_at & 1) * 2 + core,
            6 + y_at,
            10 + (x_at & 1) * 4 + y_at,
            18 + x_at * 4 + y_at,
        )
        for level, slot in enumerate(slots):
            sums[slot, rows, :] = -load_sep[:, level * BLK : (level + 1) * BLK]

    here = times_transposed(load[...], inverse[0])
    solved[...] = here
    left = beside(here)
    for q in range(8):
        matrix = stacked(coupling[0, q])
        out = dot_nt(left, jnp.concatenate([matrix, matrix], axis=1))
        index = pattern[block * 8 + q]
        slot = jnp.where(index < 6, index, 6 + ((index - 6) >> 1))
        slot = jnp.where((index >= 6) & ((index & 1) != core), slot + 34, slot)
        sums[slot] += out[:, :BLK] + out[:, BLK:]

    @pl.when(block == pl.num_programs(0) - 1)
    def _():
        mine13[...] = sums[0:10]
        theirs13[0:6] = sums[0:6]
        theirs13[6:10] = sums[40:44]
        mine45[...] = sums[10:34]
        theirs45[...] = sums[44:68]


def leaf_forward(coords, pattern, load_leaf, leaf_inverse, leaf_coupling, load_sep):
    blocks = leaf_inverse.shape[0]
    whole = lambda *shape: pl.BlockSpec(shape, lambda b, *_: (0,) * len(shape))
    outs = [(BLK, blocks * BLK), (10, BLK, BLK), (10, BLK, BLK), (24, BLK, BLK), (24, BLK, BLK)]
    return pl.pallas_call(
        leaf_forward_kernel,
        name="leaf_forward",
        out_shape=[jax.ShapeDtypeStruct(shape, F32) for shape in outs],
        grid_spec=pltpu.PrefetchScalarGridSpec(
            num_scalar_prefetch=2,
            grid=(blocks,),
            in_specs=[
                pl.BlockSpec((BLK, BLK), lambda b, *_: (0, b)),
                pl.BlockSpec((1, BLK, BLK), lambda b, *_: (b, 0, 0)),
                pl.BlockSpec((1, 8, BLK, BLK), lambda b, *_: (b, 0, 0, 0)),
                whole(COLS, 5 * BLK),
            ],
            out_specs=[pl.BlockSpec((BLK, BLK), lambda b, *_: (0, b))]
            + [whole(*shape) for shape in outs[1:]],
            scratch_shapes=[pltpu.VMEM((68, BLK, BLK), F32)],
        ),
        compiler_params=pltpu.CompilerParams(vmem_limit_bytes=VMEM_BYTES),
    )(coords, pattern, load_leaf, leaf_inverse, leaf_coupling, load_sep)


def front_parts_kernel(coords, mine, received, own, part1, part2, part3):
    for j, out in enumerate((own, part1, part2, part3)):
        rows = pl.ds(pl.multiple_of((coords[3] ^ j) * COLS, COLS), COLS)
        out[...] = mine[:, rows, :] + received[:, rows, :]


def front_parts(coords, mine, received):
    shape = (mine.shape[0], COLS, BLK)
    return call(front_parts_kernel, "front_parts", coords, [mine, received], [shape] * 4)


def level12_message_kernel(coords, own, part1, part2, part3, keep, message):
    total = (own[...] + part1[...]) + (part2[...] + part3[...])
    y_at = coords[1]
    keep[0:6] = total[0:6]
    message[0:6] = total[0:6]

    def level3(j):
        row = pl.ds(6 + (y_at ^ j), 1)
        return (own[row] + part1[row]) + (part2[row] + part3[row])

    keep[6:7] = level3(0)
    keep[7:8] = level3(3)
    message[6:7] = level3(1)
    message[7:8] = level3(2)


def level12_kernel(
    coords, keep, received, own6, core6, y6, diagonal6, solved, message, left1, level1
):
    core, y_bit = coords[0], coords[1] & 1
    members = []
    for dy in range(2):
        for dc in range(2):
            members.append(((y_bit ^ dy) * 2 + (core ^ dc), dy, core ^ dc))
    mats = (own6, core6, y6, diagonal6)
    for (index, dy, at), mat in zip(members, mats):
        source = received if dy else keep
        here = times_transposed(-source[at], mat[0])
        solved[index] = here
        left1[index] = stacked(here)
    for (index, dy, at), mat in zip(members, mats):
        acc = sum_times_transposed([left1[m] for m in range(4)], [mat[2 + m] for m in range(4)])
        rhs = -(keep[2 + index] + received[2 + index]) - fold(acc)
        solved[4 + index] = times_transposed(rhs, mat[1])
    message[0:8] = solved[0:8]
    solved[8] = keep[6] + received[6]
    message[8] = keep[7] + received[7]


def level3_kernel(
    coords, solved, received, inverse, coupling, y3, y12, y12p, mats, sems, left
):
    fetch(coupling, RUNS[3, 1], 16, mats, sems)
    core, half = coords[0], coords[1] >> 1
    for level in range(2):
        for k in range(4):
            for source, part in ((solved, half), (received, 1 - half)):
                at = level * 8 + part * 4 + k
                y12[at] = source[level * 4 + k]
                left[at] = stacked(source[level * 4 + k])
    for level in range(2):
        for y in range(4):
            y12p[level * 4 + y] = y12[level * 8 + y * 2 + core]
    fetched(coupling, RUNS[3, 1], 16, mats, sems)
    acc = sum_times_transposed([left[m] for m in range(16)], [mats[m] for m in range(16)])
    rhs = -(solved[8] + received[8]) - fold(acc)
    y3[...] = times_transposed(rhs, inverse[2])


def level4_operand_kernel(coords, y3, own, part1, part2, part3, operand, sums5):
    for p in range(8):
        operand[p, 0] = y3[...]
        operand[p, 1] = (own[p] + part1[p]) + (part2[p] + part3[p])
    sums5[...] = (own[8:24] + part1[8:24]) + (part2[8:24] + part3[8:24])


def level4_before_kernel(coords, y12, r8, c8, coupling, acc, mats, sems, left):
    fetch(coupling, RUNS[4, 1], 32, mats, sems)
    core, x_bit = coords[0], coords[2] & 1
    for level in range(2):
        for m in range(8):
            left[level * 16 + x_bit * 8 + m] = stacked(y12[level * 8 + m])
        for y in range(4):
            at = level * 16 + (1 - x_bit) * 8 + y * 2
            left[at + core] = stacked(r8[level * 4 + y])
            left[at + 1 - core] = stacked(c8[level * 4 + y])
    fetched(coupling, RUNS[4, 1], 32, mats, sems)
    acc[...] = sum_times_transposed([left[m] for m in range(32)], [mats[m] for m in range(32)])


def level4_kernel(coords, acc, mine, other, sums5, inverse, coupling, y4, operand, mats, sems, left):
    fetch(coupling, RUNS[4, 3], 16, mats, sems)
    core = coords[0]
    total = mine[0, 1]
    for p in range(1, 8):
        total = total + mine[p, 1]
    for p in range(8):
        left[p * 2 + core] = stacked(mine[p, 0])
        left[p * 2 + 1 - core] = stacked(other[p, 0])
    fetched(coupling, RUNS[4, 3], 16, mats, sems)
    terms = acc[...] + sum_times_transposed(
        [left[m] for m in range(16)], [mats[m] for m in range(16)]
    )
    here = times_transposed(-total - fold(terms), inverse[3])
    y4[...] = here
    for p in range(16):
        operand[p, 0] = here
        operand[p, 1] = sums5[p]


def level5_before_kernel(
    coords, y12, r8, c8, r24, c24, r16, c16, y3m, y3o, z3m, z3o, coupling, acc, mats, sems, left
):
    fetch(coupling, RUNS[5, 1], 96, mats, sems)
    core, x_at = coords[0], coords[2]
    for level in range(2):
        for m in range(8):
            left[level * 32 + x_at * 8 + m] = stacked(y12[level * 8 + m])
        for j, same, other in ((1, r8, c8), (3, r24, c24), (2, r16, c16)):
            for y in range(4):
                at = level * 32 + (x_at ^ j) * 8 + y * 2
                left[at + core] = stacked(same[level * 4 + y])
                left[at + 1 - core] = stacked(other[level * 4 + y])
    for half, same, other in ((x_at >> 1, y3m, y3o), (1 - (x_at >> 1), z3m, z3o)):
        for p in range(8):
            at = 64 + half * 16 + p * 2
            left[at + core] = stacked(same[p, 0])
            left[at + 1 - core] = stacked(other[p, 0])
    fetched(coupling, RUNS[5, 1], 96, mats, sems)

    def step(i, total):
        at = i * CHUNK
        return total + sum_times_transposed(
            [left[at + m] for m in range(CHUNK)], [mats[at + m] for m in range(CHUNK)]
        )

    acc[...] = lax.fori_loop(0, 96 // CHUNK, step, jnp.zeros((2 * COLS, 2 * BLK), F32))


def level5_kernel(coords, acc, mine, other, inverse, coupling, x5, operand, mats, sems, left):
    fetch(coupling, RUNS[5, 4], 32, mats, sems)
    core = coords[0]
    total = mine[0, 1]
    for p in range(1, 16):
        total = total + mine[p, 1]
    for p in range(16):
        left[p * 2 + core] = stacked(mine[p, 0])
        left[p * 2 + 1 - core] = stacked(other[p, 0])
    fetched(coupling, RUNS[5, 4], 32, mats, sems)
    terms = acc[...] + sum_times_transposed(
        [left[m] for m in range(32)], [mats[m] for m in range(32)]
    )
    solved = times_transposed(-total - fold(terms), inverse[4])
    here = times(solved, inverse[4])
    x5[...] = here
    wide = wide_left(here)
    for p in range(16):
        operand[p, 0], operand[p, 1] = two_times(wide, mats[2 * p], mats[2 * p + 1])
        operand[p, 2] = here


def level5_back_kernel(coords, x5, coupling, mine, theirs, mats, sems):
    fetch(coupling, RUNS[5, 1], 96, mats, sems)
    core = coords[0]
    wide = wide_left(x5[...])
    fetched(coupling, RUNS[5, 1], 96, mats, sems)

    def step(i, _):
        for k in range(CHUNK // 2):
            pair = i * (CHUNK // 2) + k
            at = pair * 2
            mine[pair], theirs[pair] = two_times(wide, mats[at + core], mats[at + 1 - core])
        return 0

    lax.fori_loop(0, 96 // CHUNK, step, 0)


def halves_kernel(coords, mine, received, keep, send):
    half = coords[2] >> 1
    for level in range(3):
        for out, part in ((keep, half), (send, 1 - half)):
            rows = pl.ds(level * 16 + part * 8, 8)
            out[level * 8 : level * 8 + 8] = mine[rows] + received[rows]


def level4_sum_kernel(coords, parts, own, other, x5p):
    core = coords[0]
    for out, at in ((own, core), (other, 1 - core)):
        total = parts[0, at]
        for p in range(1, 16):
            total = total + parts[p, at]
        out[...] = total
    for p in range(16):
        x5p[p] = parts[p, 2]


def level4_back_kernel(coords, y4, own, received, inverse, coupling, x4, mine, theirs, mats, sems):
    fetch(coupling, RUNS[4, 1], 48, mats, sems)
    core = coords[0]
    here = times(y4[...] - (own[...] + received[...]), inverse[3])
    x4[...] = here
    wide = wide_left(here)
    fetched(coupling, RUNS[4, 1], 48, mats, sems)
    for pair in range(24):
        mine[pair], theirs[pair] = two_times(wide, mats[2 * pair + core], mats[2 * pair + 1 - core])


def level3_operand_kernel(coords, x4, mine, received, keep, top, operand):
    for p in range(8):
        for level in range(3):
            at = level * 8 + p
            operand[p, level] = (mine[at] + received[at]) + (keep[at] + top[at])
        operand[p, 3] = x4[...]


def level3_back_kernel(
    coords, parts, y3, inverse, coupling, x3, x4p, keep, message, mats, sems, spread
):
    fetch(coupling, RUNS[3, 1], 16, mats, sems)
    core, y_at = coords[0], coords[1]
    sums = []
    for level in range(3):
        total = parts[0, level]
        for p in range(1, 8):
            total = total + parts[p, level]
        sums.append(total)
    for p in range(8):
        x4p[p] = parts[p, 3]
    here = times(y3[...] - sums[2], inverse[2])
    x3[...] = here
    wide = wide_left(here)
    fetched(coupling, RUNS[3, 1], 16, mats, sems)
    for pair in range(8):
        spread[2 * pair], spread[2 * pair + 1] = two_times(wide, mats[2 * pair], mats[2 * pair + 1])
    for level in range(2):
        spread[level * 8 + y_at * 2 + core] += sums[level]
    half = y_at >> 1
    for level in range(2):
        for out, part in ((keep, half), (message, 1 - half)):
            out[level * 4 : level * 4 + 4] = spread[pl.ds(level * 8 + part * 4, 4)]
    message[8] = here


def level3_sum_kernel(coords, keep, received, x3, message):
    message[0:8] = keep[...] + received[0:8]
    message[8] = x3[...]
    message[9] = received[8]


def level12_back_kernel(
    coords, m0, m1, m2, m3, solved, own6, core6, y6, diagonal6, own1, own2, x123, left, terms, here2
):
    core, y_at = coords[0], coords[1]
    y_bit = y_at & 1
    terms[...] = (m0[0:8] + m1[0:8]) + (m2[0:8] + m3[0:8])
    for message, dy, dc in ((m0, 0, 0), (m1, 0, 1), (m2, 1, 0), (m3, 1, 1)):
        x123[6 + (y_at ^ dy) * 2 + (core ^ dc)] = message[8]
        x123[6 + (y_at ^ dy ^ 3) * 2 + (core ^ dc)] = message[9]
    members = [
        ((y_bit ^ dy) * 2 + (core ^ dc), dy, core ^ dc) for dy in range(2) for dc in range(2)
    ]
    mats = (own6, core6, y6, diagonal6)
    for k, ((index, dy, at), mat) in enumerate(zip(members, mats)):
        here = times(solved[4 + index] - terms[4 + index], mat[1])
        x123[2 + index] = here
        if k == 0:
            own2[...] = here
        wide = wide_left(here)
        for m in range(0, 4, 2):
            first, second = two_times(wide, mat[2 + m], mat[3 + m])
            terms[m] += first
            terms[m + 1] += second
    for k in range(2):
        index, dy, at = members[k]
        here = times(solved[index] - terms[index], mats[k][0])
        x123[at] = here
        if k == 0:
            own1[...] = here


def leaf_backward_kernel(
    coords, pattern, low0, low1, low2, low3, x4m, x4o, x5m, x5o, solved, inverse, coupling, out, blocks
):
    block = pl.program_id(0)
    core, front = coords[0], coords[3]

    @pl.when(block == 0)
    def _():
        def place(index, j, value):
            high, low = split(value)
            at = pl.multiple_of((front ^ j) * COLS, COLS)
            blocks[index, pl.ds(at, COLS), :] = high
            blocks[index, pl.ds(BLK + at, COLS), :] = low

        for j, low in enumerate((low0, low1, low2, low3)):
            for a in range(14):
                place(a, j, low[a])
            for p in range(8):
                place(14 + 2 * p + core, j, x4m[j, p])
                place(15 + 2 * p - core, j, x4o[j, p])
            for p in range(16):
                place(30 + 2 * p + core, j, x5m[j, p])
                place(31 + 2 * p - core, j, x5o[j, p])

    total = None
    for q in range(0, 8, 2):
        left = jnp.concatenate([blocks[pattern[block * 8 + q + k]] for k in range(2)], axis=1)
        right = jnp.concatenate([beside(coupling[0, q + k]) for k in range(2)], axis=0)
        part = dot_nn(left, right)
        total = part if total is None else total + part
    out[...] = times(solved[...] - fold(total), inverse[0])


def leaf_backward(coords, pattern, lows, x4m, x4o, x5m, x5o, solved, leaf_inverse, leaf_coupling):
    blocks = leaf_inverse.shape[0]
    whole = lambda array: pl.BlockSpec(array.shape, lambda b, *_: (0,) * array.ndim)
    gathered = [*lows, x4m, x4o, x5m, x5o]
    return pl.pallas_call(
        leaf_backward_kernel,
        name="leaf_backward",
        out_shape=jax.ShapeDtypeStruct((BLK, blocks * BLK), F32),
        grid_spec=pltpu.PrefetchScalarGridSpec(
            num_scalar_prefetch=2,
            grid=(blocks,),
            in_specs=[whole(array) for array in gathered]
            + [
                pl.BlockSpec((BLK, BLK), lambda b, *_: (0, b)),
                pl.BlockSpec((1, BLK, BLK), lambda b, *_: (b, 0, 0)),
                pl.BlockSpec((1, 8, BLK, BLK), lambda b, *_: (b, 0, 0, 0)),
            ],
            out_specs=pl.BlockSpec((BLK, BLK), lambda b, *_: (0, b)),
            scratch_shapes=[pltpu.VMEM((62, 2 * BLK, BLK), BF16)],
        ),
        compiler_params=pltpu.CompilerParams(vmem_limit_bytes=VMEM_BYTES),
    )(coords, pattern, *gathered, solved, leaf_inverse, leaf_coupling)


def across(value, mask):
    return lax.ppermute(value, "leaf", [(i, i ^ mask) for i in range(32)])


def across_front(value, mask):
    return lax.ppermute(value, "front", [(i, i ^ mask) for i in range(4)])


def swap8(value):
    groups = [[s + c + 2 * p for p in range(8)] for s in (0, 16) for c in (0, 1)]
    return lax.all_to_all(value, "leaf", 0, 0, axis_index_groups=groups)


def swap16(value):
    groups = [[c + 2 * p for p in range(16)] for c in (0, 1)]
    return lax.all_to_all(value, "leaf", 0, 0, axis_index_groups=groups)


def local(
    load_leaf, leaf_inverse, leaf_coupling, leaf_pattern, load_sep, sep_inverse, sep_coupling
):
    leaf_at = lax.axis_index("leaf")
    coords = jnp.stack([leaf_at & 1, (leaf_at >> 1) & 3, leaf_at >> 3, lax.axis_index("front")])
    coords = coords.astype(jnp.int32)
    pattern = leaf_pattern.reshape(-1)
    one = (COLS, BLK)
    left = lambda count: pltpu.VMEM((count, 2 * COLS, BLK), BF16)

    own6 = jnp.concatenate([sep_inverse[0:2], sep_coupling[0:4]], axis=0)
    y6 = across(own6, 2)
    core6 = across(own6, 1)
    diagonal6 = across(y6, 1)
    group = [own6, core6, y6, diagonal6]

    solved_leaf, mine13, theirs13, mine45, theirs45 = leaf_forward(
        coords, pattern, load_leaf, leaf_inverse, leaf_coupling, load_sep
    )
    parts13 = front_parts(coords, mine13, across(theirs13, 1))
    parts13 = [parts13[0]] + [across_front(parts13[j], j) for j in (1, 2, 3)]
    keep, message = call(
        level12_message_kernel, "level12_message", coords, parts13, [(8, *one), (8, *one)]
    )
    solved12, message = call(
        level12_kernel,
        "level12",
        coords,
        [keep, across(message, 2), *group],
        [(9, *one), (9, *one)],
        scratch=[left(4), pltpu.VMEM((8, 128), F32)],
    )
    y3, y12, y12p = call(
        level3_kernel,
        "level3",
        coords,
        [solved12, across(message, 6), sep_inverse, sep_coupling],
        [one, (16, *one), (8, *one)],
        in_any=(3,),
        scratch=[*matrices(16), left(16)],
    )
    parts45 = front_parts(coords, mine45, across(theirs45, 1))
    parts45 = [parts45[0]] + [across_front(parts45[j], j) for j in (1, 2, 3)]
    operand, sums5 = call(
        level4_operand_kernel, "level4_operand", coords, [y3, *parts45], [(8, 2, *one), (16, *one)]
    )
    y3m = swap8(operand)
    r8 = across(y12p, 8)
    c8 = across(r8, 1)
    y3o = across(y3m, 1)
    (acc4,) = call(
        level4_before_kernel,
        "level4_before",
        coords,
        [y12, r8, c8, sep_coupling],
        [(2 * COLS, 2 * BLK)],
        in_any=(3,),
        scratch=[*matrices(32), left(32)],
    )
    y4, operand = call(
        level4_kernel,
        "level4",
        coords,
        [acc4, y3m, y3o, sums5, sep_inverse, sep_coupling],
        [one, (16, 2, *one)],
        in_any=(5,),
        scratch=[*matrices(16), left(16)],
    )
    y4m = swap16(operand)
    r24 = across(y12p, 24)
    r16 = across(r8, 24)
    c24 = across(r24, 1)
    c16 = across(r16, 1)
    z3m = across(y3m, 24)
    z3o = across(z3m, 1)
    y4o = across(y4m, 1)
    (acc5,) = call(
        level5_before_kernel,
        "level5_before",
        coords,
        [y12, r8, c8, r24, c24, r16, c16, y3m, y3o, z3m, z3o, sep_coupling],
        [(2 * COLS, 2 * BLK)],
        in_any=(11,),
        scratch=[*matrices(96), left(96)],
    )
    x5, operand = call(
        level5_kernel,
        "level5",
        coords,
        [acc5, y4m, y4o, sep_inverse, sep_coupling],
        [one, (16, 3, *one)],
        in_any=(4,),
        scratch=[*matrices(32), left(32)],
    )
    parts4 = swap16(operand)
    mine, theirs = call(
        level5_back_kernel,
        "level5_back",
        coords,
        [x5, sep_coupling],
        [(48, *one), (48, *one)],
        in_any=(1,),
        scratch=matrices(96),
    )
    keep_top, send_top = call(
        halves_kernel, "halves", coords, [mine, across(theirs, 1)], [(24, *one), (24, *one)]
    )
    top = across(send_top, 24)
    own, other, x5p = call(
        level4_sum_kernel, "level4_sum", coords, [parts4], [one, one, (16, *one)]
    )
    x4, mine, theirs = call(
        level4_back_kernel,
        "level4_back",
        coords,
        [y4, own, across(other, 1), sep_inverse, sep_coupling],
        [one, (24, *one), (24, *one)],
        in_any=(4,),
        scratch=matrices(48),
    )
    (operand,) = call(
        level3_operand_kernel,
        "level3_operand",
        coords,
        [x4, mine, across(theirs, 1), keep_top, top],
        [(8, 4, *one)],
    )
    parts3 = swap8(operand)
    x3, x4p, keep, message = call(
        level3_back_kernel,
        "level3_back",
        coords,
        [parts3, y3, sep_inverse, sep_coupling],
        [one, (8, *one), (8, *one), (9, *one)],
        in_any=(3,),
        scratch=[*matrices(16), pltpu.VMEM((16, *one), F32)],
    )
    (message,) = call(
        level3_sum_kernel, "level3_sum", coords, [keep, across(message, 6), x3], [(10, *one)]
    )
    x1, x2, x123 = call(
        level12_back_kernel,
        "level12_back",
        coords,
        [message, across(message, 1), across(message, 2), across(message, 3), solved12, *group],
        [one, one, (14, *one)],
        scratch=[left(4), pltpu.VMEM((8, *one), F32), pltpu.VMEM((8, 128), F32)],
    )
    lows = [x123] + [across_front(x123, j) for j in (1, 2, 3)]
    x4m = jnp.stack([x4p] + [across_front(x4p, j) for j in (1, 2, 3)])
    x5m = jnp.stack([x5p] + [across_front(x5p, j) for j in (1, 2, 3)])
    solution_leaf = leaf_backward(
        coords,
        pattern,
        lows,
        x4m,
        across(x4m, 1),
        x5m,
        across(x5m, 1),
        solved_leaf,
        leaf_inverse,
        leaf_coupling,
    )
    solution_sep = jnp.concatenate([x1, x2, x3, x4, x5], axis=1)
    return solution_leaf, solution_sep


def solution(mesh):
    return jax.shard_map(
        local,
        mesh=mesh,
        in_specs=(
            P(None, ("leaf", "front")),
            P(("leaf", "front"), None, None),
            P(("leaf", "front"), None, None, None),
            P(("leaf", "front"), None),
            P("front", "leaf"),
            P("leaf", None, None),
            P("leaf", None, None),
        ),
        out_specs=(P(None, ("leaf", "front")), P("front", "leaf")),
        check_vma=False,
    )
```

```python
import jax
import jax.numpy as jnp
from jax import lax
from jax.experimental import pallas as pl
from jax.experimental.pallas import tpu as pltpu
from jax.sharding import PartitionSpec as P

F32 = jnp.float32
BF16 = jnp.bfloat16
BLK = 128
COLS = 32
VMEM_BYTES = 32 * 1024 * 1024
LARGE_VMEM_BYTES = 48 * 1024 * 1024
RUNS = {(2, 1): 0, (3, 1): 4, (3, 2): 12, (4, 1): 20, (4, 2): 36, (4, 3): 52}
RUNS |= {(5, 1): 68, (5, 2): 100, (5, 3): 132, (5, 4): 164}
CHUNK = 8


def split(value):
    high = value.astype(BF16)
    low = (value - high.astype(F32)).astype(BF16)
    return high, low


def stacked(value):
    return jnp.concatenate(split(value), axis=0)


def beside(value):
    return jnp.concatenate(split(value), axis=1)


def dot_nt(left, right):
    return lax.dot_general(left, right, (((1,), (1,)), ((), ())), preferred_element_type=F32)


def dot_nn(left, right):
    return lax.dot_general(left, right, (((1,), (0,)), ((), ())), preferred_element_type=F32)


def fold(terms):
    rows = terms.shape[0] // 2
    return (terms[:rows, :BLK] + terms[:rows, BLK:]) + (terms[rows:, :BLK] + terms[rows:, BLK:])


def times_transposed(value, matrix):
    return fold(dot_nt(stacked(value), stacked(matrix)))


def times(value, matrix):
    return fold(dot_nn(stacked(value), beside(matrix)))


def sum_times_transposed(lefts, matrices):
    total = None
    for k in range(0, len(lefts), 2):
        left = jnp.concatenate([lefts[k], lefts[k + 1]], axis=1)
        right = jnp.concatenate([stacked(matrices[k]), stacked(matrices[k + 1])], axis=1)
        part = dot_nt(left, right)
        total = part if total is None else total + part
    return total


def wide_left(value):
    both = stacked(value)
    return jnp.concatenate([both, both], axis=1)


def two_times(left, first, second):
    right = jnp.concatenate([stacked(first), stacked(second)], axis=1)
    out = dot_nn(left, right)
    rows = out.shape[0] // 2
    out = out[:rows] + out[rows:]
    return out[:, :BLK], out[:, BLK:]


def cost(us):
    return pl.CostEstimate(
        flops=int(us * 1e8), bytes_accessed=int(us * 3e5), transcendentals=0
    )


def call(
    body, name, coords, inputs, outs, us=1.0, in_hbm=(), after=(), through=(), scratch=(), limit=VMEM_BYTES
):
    count, results = len(inputs), len(outs)
    extra = len(after) + len(through)

    def kernel(coords_ref, *refs):
        refs = list(refs)
        del refs[count + extra + results : count + extra + results + len(through)]
        del refs[count : count + extra]
        body(coords_ref, *refs)

    anywhere = pl.BlockSpec(memory_space=pl.ANY)
    hbm = pl.BlockSpec(memory_space=pltpu.HBM)
    vmem = pl.BlockSpec(memory_space=pltpu.VMEM)
    specs = [hbm if k in in_hbm else vmem for k in range(count)] + [anywhere] * extra
    first = 1 + count + len(after)
    return pl.pallas_call(
        kernel,
        name=name,
        out_shape=[jax.ShapeDtypeStruct(shape, F32) for shape in outs]
        + [jax.ShapeDtypeStruct(array.shape, array.dtype) for array in through],
        grid_spec=pltpu.PrefetchScalarGridSpec(
            num_scalar_prefetch=1,
            grid=(1,),
            in_specs=specs,
            out_specs=[vmem] * results + [anywhere] * len(through),
            scratch_shapes=list(scratch),
        ),
        input_output_aliases={first + k: results + k for k in range(len(through))},
        compiler_params=pltpu.CompilerParams(vmem_limit_bytes=limit),
        cost_estimate=cost(us),
    )(coords, *inputs, *after, *through)


def fetch(source, first, count, target, sems):
    for k in range(0, count, CHUNK):
        pltpu.make_async_copy(
            source.at[pl.ds(first + k, CHUNK)], target.at[pl.ds(k, CHUNK)], sems.at[k // CHUNK]
        ).start()


def fetched(source, first, target, sems, k):
    pltpu.make_async_copy(
        source.at[pl.ds(first + k * CHUNK, CHUNK)], target.at[pl.ds(k * CHUNK, CHUNK)], sems.at[k]
    ).wait()


def matrices(count):
    return [pltpu.VMEM((count, BLK, BLK), F32), pltpu.SemaphoreType.DMA((count // CHUNK,))]


PER_COPY = 2


def leaf_copies(load, inverse, coupling, loads, inverses, couplings, sems, blocks):
    copies = [
        pltpu.make_async_copy(load, loads, sems.at[0]),
        pltpu.make_async_copy(inverse, inverses, sems.at[1]),
    ]
    for k in range(blocks // PER_COPY):
        part = pl.ds(k * PER_COPY, PER_COPY)
        copies.append(
            pltpu.make_async_copy(coupling.at[part], couplings.at[part], sems.at[2 + k])
        )
    return copies


def leaf_forward_kernel(
    coords, pattern, load, inverse, coupling, load_sep,
    mine13, theirs13, mine45, theirs45,
    loads, inverses, couplings, load_seps, solved, sums, columns, sems, sep_sem,
):
    blocks = couplings.shape[0]
    core, y_at, x_at, front = coords[0], coords[1], coords[2], coords[3]
    copies = leaf_copies(load, inverse, coupling, loads, inverses, couplings, sems, blocks)
    sep_copy = pltpu.make_async_copy(load_sep, load_seps, sep_sem)
    sep_copy.start()
    for copy in copies:
        copy.start()
    sums[...] = jnp.zeros_like(sums)
    columns[...] = jnp.zeros_like(columns)
    rows = pl.ds(pl.multiple_of(front * COLS, COLS), COLS)
    slots = (
        core,
        2 + (y_at & 1) * 2 + core,
        6 + y_at,
        10 + (x_at & 1) * 4 + y_at,
        18 + x_at * 4 + y_at,
    )
    sep_copy.wait()
    for level, slot in enumerate(slots):
        columns[rows, :] = -load_seps[:, level * BLK : (level + 1) * BLK]
        sums[slot] = columns[...].T
    copies[0].wait()
    copies[1].wait()
    for b in range(blocks):
        turned = fold(
            dot_nt(stacked(inverses[b]), stacked(loads[:, b * BLK : (b + 1) * BLK]))
        )
        solved[b] = beside(turned)

    for k in range(blocks // PER_COPY):
        copies[2 + k].wait()
        for b in range(k * PER_COPY, (k + 1) * PER_COPY):
            right = jnp.concatenate([solved[b], solved[b]], axis=0)
            left = jnp.concatenate([beside(couplings[b, q]) for q in range(8)], axis=0)
            out = dot_nn(left, right)
            out = out[:, :BLK] + out[:, BLK:]
            for q in range(8):
                index = pattern[b, q]
                slot = jnp.where(index < 6, index, 6 + ((index - 6) >> 1))
                slot = jnp.where((index >= 6) & ((index & 1) != core), slot + 34, slot)
                sums[slot] += out[q * BLK : (q + 1) * BLK]

    mine13[...] = sums[0:10]
    theirs13[0:6] = sums[0:6]
    theirs13[6:10] = sums[40:44]
    mine45[...] = sums[10:34]
    theirs45[...] = sums[44:68]


def leaf_forward(coords, pattern, load_leaf, leaf_inverse, leaf_coupling, load_sep):
    blocks = leaf_inverse.shape[0]
    outs = [(10, BLK, BLK), (10, BLK, BLK), (24, BLK, BLK), (24, BLK, BLK)]
    vmem = pl.BlockSpec(memory_space=pltpu.VMEM)
    return pl.pallas_call(
        leaf_forward_kernel,
        name="leaf_forward",
        out_shape=[jax.ShapeDtypeStruct(shape, F32) for shape in outs],
        grid_spec=pltpu.PrefetchScalarGridSpec(
            num_scalar_prefetch=2,
            grid=(1,),
            in_specs=[pl.BlockSpec(memory_space=pltpu.HBM)] * 4,
            out_specs=[vmem] * 4,
            scratch_shapes=[
                pltpu.VMEM(load_leaf.shape, F32),
                pltpu.VMEM(leaf_inverse.shape, F32),
                pltpu.VMEM(leaf_coupling.shape, F32),
                pltpu.VMEM(load_sep.shape, F32),
                pltpu.VMEM((blocks, BLK, 2 * BLK), BF16),
                pltpu.VMEM((68, BLK, BLK), F32),
                pltpu.VMEM((BLK, BLK), F32),
                pltpu.SemaphoreType.DMA((2 + blocks // PER_COPY,)),
                pltpu.SemaphoreType.DMA,
            ],
        ),
        compiler_params=pltpu.CompilerParams(vmem_limit_bytes=LARGE_VMEM_BYTES),
        cost_estimate=cost(6),
    )(coords, pattern, load_leaf, leaf_inverse, leaf_coupling, load_sep)


def front_parts(coords, mine, received, cuts, through=(), after=()):
    def kernel(coords_ref, mine_ref, received_ref, *refs):
        outs, rows_of = refs[:-1], refs[-1]
        for k in range(mine.shape[0]):
            rows_of[k] = (mine_ref[k] + received_ref[k]).T
        for j in range(4):
            rows = pl.ds(pl.multiple_of((coords_ref[3] ^ j) * COLS, COLS), COLS)
            for c in range(len(cuts) - 1):
                outs[c * 4 + j][...] = rows_of[cuts[c] : cuts[c + 1], rows, :]

    counts = [cuts[c + 1] - cuts[c] for c in range(len(cuts) - 1)]
    return call(
        kernel,
        "front_parts",
        coords,
        [mine, received],
        [(count, COLS, BLK) for count in counts for _ in range(4)],
        after=after,
        through=through,
        scratch=[pltpu.VMEM(mine.shape, F32)],
    )


def preload(coords, sources, us=2.0, after=()):
    def kernel(coords_ref, *refs):
        count = len(sources)
        copies = []
        for k, (array, first, size) in enumerate(sources):
            part = refs[k].at[pl.ds(first, size)]
            copies.append(pltpu.make_async_copy(part, refs[count + k], refs[-1].at[k]))
            copies[-1].start()
        for copy in copies:
            copy.wait()

    return call(
        kernel,
        "preload",
        coords,
        [array for array, _, _ in sources],
        [(size, BLK, BLK) for _, _, size in sources],
        us=us,
        in_hbm=tuple(range(len(sources))),
        after=after,
        scratch=[pltpu.SemaphoreType.DMA((len(sources),))],
        limit=LARGE_VMEM_BYTES,
    )


def level12_message_kernel(coords, own, part1, part2, part3, keep, message):
    total = (own[...] + part1[...]) + (part2[...] + part3[...])
    y_at = coords[1]
    keep[0:6] = total[0:6]
    message[0:6] = total[0:6]

    def level3(j):
        row = pl.ds(6 + (y_at ^ j), 1)
        return (own[row] + part1[row]) + (part2[row] + part3[row])

    keep[6:7] = level3(0)
    keep[7:8] = level3(3)
    message[6:7] = level3(1)
    message[7:8] = level3(2)


def level12_kernel(
    coords, keep, received, own6, core6, y6, diagonal6, solved, message, left1, level1
):
    core, y_bit = coords[0], coords[1] & 1
    members = []
    for dy in range(2):
        for dc in range(2):
            members.append(((y_bit ^ dy) * 2 + (core ^ dc), dy, core ^ dc))
    mats = (own6, core6, y6, diagonal6)
    for (index, dy, at), mat in zip(members, mats):
        source = received if dy else keep
        here = times_transposed(-source[at], mat[0])
        solved[index] = here
        left1[index] = stacked(here)
    for (index, dy, at), mat in zip(members, mats):
        acc = sum_times_transposed([left1[m] for m in range(4)], [mat[2 + m] for m in range(4)])
        rhs = -(keep[2 + index] + received[2 + index]) - fold(acc)
        solved[4 + index] = times_transposed(rhs, mat[1])
    message[0:8] = solved[0:8]
    solved[8] = keep[6] + received[6]
    message[8] = keep[7] + received[7]


def level3_kernel(coords, solved, received, sums4, inverse, mats, y3, operand, left):
    core, y_at = coords[0], coords[1]
    half = y_at >> 1
    own = (y_at & 1) * 2 + core
    for level in range(2):
        for k in range(4):
            for source, part in ((solved, half), (received, 1 - half)):
                left[level * 8 + part * 4 + k] = stacked(source[level * 4 + k])
    acc = sum_times_transposed([left[m] for m in range(16)], [mats[m] for m in range(16)])
    rhs = -(solved[8] + received[8]) - fold(acc)
    here = times_transposed(rhs, inverse[2])
    y3[...] = here
    for p in range(16):
        operand[p, 0] = solved[own]
        operand[p, 1] = solved[4 + own]
        operand[p, 2] = here
        operand[p, 3] = sums4[p]


def level4_sums_kernel(coords, own, part1, part2, part3, sums4):
    half = coords[2] >> 1
    sums4[pl.ds((1 - half) * 8, 8)] = jnp.zeros((8, COLS, BLK), F32)
    sums4[pl.ds(half * 8, 8)] = (own[...] + part1[...]) + (part2[...] + part3[...])


def level5_sums_kernel(coords, own, part1, part2, part3, sums5):
    sums5[...] = (own[...] + part1[...]) + (part2[...] + part3[...])


def level4_kernel(
    coords, mine, other, sums5, inverse, mats, y4, operand, left
):
    core, half = coords[0], coords[2] >> 1
    total = mine[half * 8, 3]
    for p in range(1, 8):
        total = total + mine[half * 8 + p, 3]
    for level in range(3):
        for p in range(8):
            at = level * 16 + p * 2
            left[at + core] = stacked(mine[half * 8 + p, level])
            left[at + 1 - core] = stacked(other[half * 8 + p, level])
    terms = sum_times_transposed([left[m] for m in range(48)], [mats[m] for m in range(48)])
    here = times_transposed(-total - fold(terms), inverse[3])
    y4[...] = here
    for p in range(16):
        operand[p, 0] = here
        operand[p, 1] = sums5[p]


def add_products(coupling, first, count, start, acc, mats, sems, left):
    def step(i, total):
        fetched(coupling, first, mats, sems, i)
        at = i * CHUNK
        return total + sum_times_transposed(
            [left[at + m] for m in range(CHUNK)], [mats[at + m] for m in range(CHUNK)]
        )

    acc[...] = lax.fori_loop(0, count // CHUNK, step, start)


def level5_before_kernel(coords, mine, other, coupling, acc, mats54, mats, sems, left, sem):
    fetch(coupling, RUNS[5, 1], 96, mats, sems)
    last = pltpu.make_async_copy(coupling.at[pl.ds(RUNS[5, 4], 32)], mats54, sem)
    last.start()
    core = coords[0]
    for level in range(3):
        for p in range(16):
            at = level * 32 + p * 2
            left[at + core] = stacked(mine[p, level])
            left[at + 1 - core] = stacked(other[p, level])
    start = jnp.zeros((2 * COLS, 2 * BLK), F32)
    add_products(coupling, RUNS[5, 1], 96, start, acc, mats, sems, left)
    last.wait()


def level5_kernel(coords, acc, mine, other, inverse, mats, x5, own, theirs, left, pair):
    core = coords[0]
    total = mine[0, 1]
    for p in range(1, 16):
        total = total + mine[p, 1]
    for p in range(16):
        left[p * 2 + core] = stacked(mine[p, 0])
        left[p * 2 + 1 - core] = stacked(other[p, 0])
    terms = acc[...] + sum_times_transposed(
        [left[m] for m in range(32)], [mats[m] for m in range(32)]
    )
    solved = times_transposed(-total - fold(terms), inverse[4])
    here = times(solved, inverse[4])
    x5[...] = here
    wide = wide_left(here)
    for p in range(16):
        pair[2 * p], pair[2 * p + 1] = two_times(wide, mats[2 * p], mats[2 * p + 1])
    for p in range(16):
        own[p] = pair[2 * p + core]
        theirs[p] = pair[2 * p + 1 - core]


def level4_operand_kernel(coords, x5, own, received, operand):
    for p in range(16):
        operand[p, 0] = own[p] + received[p]
        operand[p, 1] = x5[...]


def level5_back_kernel(coords, x5, coupling, spread, mats4, mats, sems, sem):
    fetch(coupling, RUNS[5, 1], 96, mats, sems)
    last = pltpu.make_async_copy(coupling.at[pl.ds(RUNS[4, 1], 48)], mats4, sem)
    last.start()
    wide = wide_left(x5[...])

    def step(i, _):
        fetched(coupling, RUNS[5, 1], mats, sems, i)
        for k in range(0, CHUNK, 2):
            at = i * CHUNK + k
            spread[at], spread[at + 1] = two_times(wide, mats[at], mats[at + 1])
        return 0

    lax.fori_loop(0, 96 // CHUNK, step, 0)
    last.wait()


def level4_back_kernel(coords, parts, y4, spread, inverse, mats, x4, x5p, mine, theirs, all4):
    core, half = coords[0], coords[2] >> 1
    total = parts[0, 0]
    for p in range(1, 16):
        total = total + parts[p, 0]
    for p in range(16):
        x5p[p] = parts[p, 1]
    here = times(y4[...] - total, inverse[3])
    x4[...] = here
    wide = wide_left(here)
    for level in range(3):
        for pair in range(16):
            mine[pair, level] = spread[level * 32 + pair * 2 + core]
            theirs[pair, level] = spread[level * 32 + pair * 2 + 1 - core]
        for pair in range(8):
            at = level * 16 + pair * 2
            all4[0], all4[1] = two_times(wide, mats[at], mats[at + 1])
            mine[half * 8 + pair, level] += all4[core]
            theirs[half * 8 + pair, level] += all4[1 - core]


def level3_operand_kernel(coords, x4, mine, received, operand):
    for p in range(16):
        operand[p, 0:3] = mine[p] + received[p]
        operand[p, 3] = x4[...]


def level3_back_kernel(coords, parts, y3, inverse, mats, x3, x4p, mine, theirs, spread):
    core, y_at = coords[0], coords[1]
    sums = []
    for level in range(3):
        total = parts[0, level]
        for p in range(1, 16):
            total = total + parts[p, level]
        sums.append(total)
    for p in range(8):
        x4p[p] = parts[(coords[2] >> 1) * 8 + p, 3]
    here = times(y3[...] - sums[2], inverse[2])
    x3[...] = here
    wide = wide_left(here)
    for pair in range(8):
        spread[2 * pair], spread[2 * pair + 1] = two_times(wide, mats[2 * pair], mats[2 * pair + 1])
    for level in range(2):
        spread[level * 8 + y_at * 2 + core] += sums[level]
    for pair in range(8):
        mine[pair] = spread[2 * pair + core]
        theirs[pair] = spread[2 * pair + 1 - core]


def pair_message_kernel(coords, mine, received, x3, keep, message):
    half = coords[1] >> 1
    for level in range(2):
        for out, part in ((keep, half), (message, 1 - half)):
            rows = pl.ds(level * 4 + part * 2, 2)
            out[level * 2 : level * 2 + 2] = mine[rows] + received[rows]
    message[4] = x3[...]


def pair_sum_kernel(coords, keep, received, x3, message):
    message[0:4] = keep[...] + received[0:4]
    message[4] = x3[...]
    message[5] = received[4]


def pair_total_kernel(coords, message, received, out):
    out[0:4] = message[0:4] + received[0:4]
    out[4:6] = message[4:6]
    out[6:8] = received[4:6]


def level12_back_kernel(
    coords, mine, other, solved, own6, core6, y6, diagonal6, own1, own2, x123, terms
):
    core, y_at = coords[0], coords[1]
    y_bit = y_at & 1
    for source, parity in ((mine, core), (other, 1 - core)):
        for level in range(2):
            for y in range(2):
                terms[level * 4 + y * 2 + parity] = source[level * 2 + y]
        for k, dy in enumerate((0, 3, 1, 2)):
            x123[6 + (y_at ^ dy) * 2 + parity] = source[4 + k]
    members = [
        ((y_bit ^ dy) * 2 + (core ^ dc), dy, core ^ dc) for dy in range(2) for dc in range(2)
    ]
    mats = (own6, core6, y6, diagonal6)
    for k, ((index, dy, at), mat) in enumerate(zip(members, mats)):
        here = times(solved[4 + index] - terms[4 + index], mat[1])
        x123[2 + index] = here
        if k == 0:
            own2[...] = here
        wide = wide_left(here)
        for m in range(0, 4, 2):
            first, second = two_times(wide, mat[2 + m], mat[3 + m])
            terms[m] += first
            terms[m + 1] += second
    for k in range(2):
        index, dy, at = members[k]
        here = times(solved[index] - terms[index], mats[k][0])
        x123[at] = here
        if k == 0:
            own1[...] = here


LOW = 14
AT_ONCE = 4


def pack_kernel(coords, part0, part1, part2, part3, out):
    for j, part in enumerate((part0, part1, part2, part3)):
        out[j] = part[...]


def pack(coords, parts):
    return call(pack_kernel, "pack", coords, parts, [(4, *parts[0].shape)])[0]


def place(blocks, index, front, j, value):
    high, low = split(value)
    at = pl.multiple_of((front ^ j) * COLS, COLS)
    blocks[index, pl.ds(at, COLS), :] = high
    blocks[index, pl.ds(BLK + at, COLS), :] = low


def leaf_high_kernel(
    coords, pattern, load, inverse, coupling, x4m, x4o, x5m, x5o,
    rhs, couplings, items,
    loads, inverses, blocks, sems,
):
    count = couplings.shape[0]
    core, front = coords[0], coords[3]
    copies = leaf_copies(load, inverse, coupling, loads, inverses, couplings, sems, count)
    for copy in copies:
        copy.start()

    def note(i, found):
        items[1 + found] = i
        return found + (pattern[i >> 3, i & 7] < LOW).astype(jnp.int32)

    items[0] = lax.fori_loop(0, count * 8, note, jnp.int32(0))
    blocks[48] = jnp.zeros((2 * BLK, BLK), BF16)
    for j in range(4):
        for p in range(8):
            place(blocks, 2 * p + core, front, j, x4m[j, p])
            place(blocks, 2 * p + 1 - core, front, j, x4o[j, p])
        for p in range(16):
            place(blocks, 16 + 2 * p + core, front, j, x5m[j, p])
            place(blocks, 16 + 2 * p + 1 - core, front, j, x5o[j, p])
    copies[0].wait()
    copies[1].wait()
    for k in range(count // PER_COPY):
        copies[2 + k].wait()
        for b in range(k * PER_COPY, (k + 1) * PER_COPY):
            here = times_transposed(loads[:, b * BLK : (b + 1) * BLK], inverses[b])
            total = None
            for q in range(0, 8, 2):
                indices = [pattern[b, q + k2] for k2 in range(2)]
                chosen = [jnp.where(index < LOW, 48, index - LOW) for index in indices]
                left = jnp.concatenate([blocks[c] for c in chosen], axis=1)
                right = jnp.concatenate([beside(couplings[b, q + k2]) for k2 in range(2)], axis=0)
                part = dot_nn(left, right)
                total = part if total is None else total + part
            rhs[b] = here - fold(total)


def leaf_high(coords, pattern, load_leaf, leaf_inverse, leaf_coupling, gathered):
    blocks = leaf_inverse.shape[0]
    vmem = pl.BlockSpec(memory_space=pltpu.VMEM)
    return pl.pallas_call(
        leaf_high_kernel,
        name="leaf_high",
        out_shape=[
            jax.ShapeDtypeStruct((blocks, BLK, BLK), F32),
            jax.ShapeDtypeStruct(leaf_coupling.shape, F32),
            jax.ShapeDtypeStruct((blocks * 8 + 2,), jnp.int32),
        ],
        grid_spec=pltpu.PrefetchScalarGridSpec(
            num_scalar_prefetch=2,
            grid=(1,),
            in_specs=[pl.BlockSpec(memory_space=pltpu.HBM)] * 3 + [vmem] * 4,
            out_specs=[vmem, vmem, pl.BlockSpec(memory_space=pltpu.SMEM)],
            scratch_shapes=[
                pltpu.VMEM(load_leaf.shape, F32),
                pltpu.VMEM(leaf_inverse.shape, F32),
                pltpu.VMEM((49, 2 * BLK, BLK), BF16),
                pltpu.SemaphoreType.DMA((2 + blocks // PER_COPY,)),
            ],
        ),
        compiler_params=pltpu.CompilerParams(vmem_limit_bytes=VMEM_BYTES),
        cost_estimate=cost(8),
    )(coords, pattern, load_leaf, leaf_inverse, leaf_coupling, *gathered)


def leaf_low_kernel(
    coords, pattern, items, low0, low1, low2, low3, rhs, inverse, couplings,
    out,
    blocks, acc, solved, sems,
):
    front, count = coords[3], items[0]
    acc[...] = rhs[...]
    blocks[LOW] = jnp.zeros((2 * BLK, BLK), BF16)
    for j, low in enumerate((low0, low1, low2, low3)):
        for a in range(LOW):
            place(blocks, a, front, j, low[a])

    def step(t, _):
        for k in range(AT_ONCE):
            at = t * AT_ONCE + k
            item = jnp.where(at < count, items[1 + jnp.minimum(at, count)], 0)
            index = jnp.where(at < count, pattern[item >> 3, item & 7], LOW)
            right = beside(couplings[item >> 3, item & 7])
            acc[item >> 3] -= fold(dot_nn(blocks[index], right))
        return 0

    lax.fori_loop(0, (count + AT_ONCE - 1) // AT_ONCE, step, 0)
    copies = []
    for b in range(rhs.shape[0]):
        solved[b] = times(acc[b], inverse[b])
        copies.append(
            pltpu.make_async_copy(solved.at[b], out.at[:, b * BLK : (b + 1) * BLK], sems.at[b])
        )
        copies[-1].start()
    for copy in copies:
        copy.wait()


def leaf_low(coords, pattern, items, lows, rhs, leaf_inverse, couplings):
    blocks = leaf_inverse.shape[0]
    vmem = pl.BlockSpec(memory_space=pltpu.VMEM)
    return pl.pallas_call(
        leaf_low_kernel,
        name="leaf_low",
        out_shape=jax.ShapeDtypeStruct((BLK, blocks * BLK), F32),
        grid_spec=pltpu.PrefetchScalarGridSpec(
            num_scalar_prefetch=3,
            grid=(1,),
            in_specs=[vmem] * 7,
            out_specs=pl.BlockSpec(memory_space=pltpu.HBM),
            scratch_shapes=[
                pltpu.VMEM((LOW + 1, 2 * BLK, BLK), BF16),
                pltpu.VMEM((blocks, BLK, BLK), F32),
                pltpu.VMEM((blocks, BLK, BLK), F32),
                pltpu.SemaphoreType.DMA((blocks,)),
            ],
        ),
        compiler_params=pltpu.CompilerParams(vmem_limit_bytes=VMEM_BYTES),
        cost_estimate=cost(4),
    )(coords, pattern, items, *lows, rhs, leaf_inverse, couplings)


def across(value, mask):
    return lax.ppermute(value, "leaf", [(i, i ^ mask) for i in range(32)])


def across_front(value, mask):
    return lax.ppermute(value, "front", [(i, i ^ mask) for i in range(4)])


def swap16(value):
    groups = [[c + 2 * p for p in range(16)] for c in (0, 1)]
    return lax.all_to_all(value, "leaf", 0, 0, axis_index_groups=groups)


def local(
    load_leaf, leaf_inverse, leaf_coupling, leaf_pattern, load_sep, sep_inverse, sep_coupling
):
    leaf_at = lax.axis_index("leaf")
    coords = jnp.stack([leaf_at & 1, (leaf_at >> 1) & 3, leaf_at >> 3, lax.axis_index("front")])
    coords = coords.astype(jnp.int32)
    pattern = leaf_pattern
    one = (COLS, BLK)
    wide = (2 * COLS, 2 * BLK)
    left = lambda count: pltpu.VMEM((count, 2 * COLS, BLK), BF16)
    own6 = jnp.concatenate([sep_inverse[0:2], sep_coupling[0:4]], axis=0)
    mine13, theirs13, mine45, theirs45 = leaf_forward(
        coords, pattern, load_leaf, leaf_inverse, leaf_coupling, load_sep
    )
    *parts13, theirs45, own6 = front_parts(
        coords, mine13, across(theirs13, 1), (0, 10), through=[theirs45, own6]
    )
    parts13 = [parts13[0]] + [across_front(parts13[j], j) for j in (1, 2, 3)]
    y6 = across(own6, 2)
    core6 = across(own6, 1)
    parts45 = front_parts(coords, mine45, across(theirs45, 1), (0, 8, 24))
    parts4, parts5 = parts45[0:4], parts45[4:8]
    inverses, mats3 = preload(
        coords,
        [(sep_inverse, 0, 5), (sep_coupling, RUNS[3, 1], 16)],
        after=[parts45[0]],
    )
    keep, message, y6 = call(
        level12_message_kernel,
        "level12_message",
        coords,
        parts13,
        [(8, *one), (8, *one)],
        after=[parts45[0], mats3],
        through=[y6],
    )
    diagonal6 = across(y6, 1)
    group = [own6, core6, y6, diagonal6]
    parts4 = [parts4[0]] + [across_front(parts4[j], j) for j in (1, 2, 3)]
    solved12, message = call(
        level12_kernel,
        "level12",
        coords,
        [keep, across(message, 2), *group],
        [(9, *one), (9, *one)],
        us=2,
        scratch=[left(4), pltpu.VMEM((8, 128), F32)],
    )
    (sums4,) = call(
        level4_sums_kernel, "level4_sums", coords, parts4, [(16, *one)]
    )
    parts5 = [parts5[0]] + [across_front(parts5[j], j) for j in (1, 2, 3)]
    y3, operand = call(
        level3_kernel,
        "level3",
        coords,
        [solved12, across(message, 6), sums4, inverses, mats3],
        [one, (16, 4, *one)],
        us=2,
        scratch=[left(16)],
    )
    low_mine = swap16(operand)
    (mats4,) = preload(coords, [(sep_coupling, RUNS[4, 1], 48)], us=3, after=[y3])
    (sums5,) = call(
        level5_sums_kernel, "level5_sums", coords, parts5, [(16, *one)]
    )
    low_mine, mats4, sums5 = lax.optimization_barrier((low_mine, mats4, sums5))
    low_other = across(low_mine, 1)
    y4, operand = call(
        level4_kernel,
        "level4",
        coords,
        [low_mine, low_other, sums5, inverses, mats4],
        [one, (16, 2, *one)],
        us=3,
        scratch=[left(48)],
    )
    y4m = swap16(operand)
    acc5, mats54 = call(
        level5_before_kernel,
        "level5_before",
        coords,
        [low_mine, low_other, sep_coupling],
        [wide, (32, BLK, BLK)],
        us=6,
        in_hbm=(2,),
        scratch=[*matrices(96), left(96), pltpu.SemaphoreType.DMA],
        limit=LARGE_VMEM_BYTES,
    )
    y4m, acc5, mats54 = lax.optimization_barrier((y4m, acc5, mats54))
    y4o = across(y4m, 1)
    x5, own4, theirs4 = call(
        level5_kernel,
        "level5",
        coords,
        [acc5, y4m, y4o, inverses, mats54],
        [one, (16, *one), (16, *one)],
        us=4,
        scratch=[left(32), pltpu.VMEM((32, *one), F32)],
    )
    (operand,) = call(
        level4_operand_kernel,
        "level4_operand",
        coords,
        [x5, own4, across(theirs4, 1)],
        [(16, 2, *one)],
    )
    sums4 = swap16(operand)
    spread, mats4 = call(
        level5_back_kernel,
        "level5_back",
        coords,
        [x5, sep_coupling],
        [(96, *one), (48, BLK, BLK)],
        us=6,
        in_hbm=(1,),
        scratch=[*matrices(96), pltpu.SemaphoreType.DMA],
        limit=LARGE_VMEM_BYTES,
    )
    x4, x5p, mine, theirs = call(
        level4_back_kernel,
        "level4_back",
        coords,
        [sums4, y4, spread, inverses, mats4],
        [one, (16, *one), (16, 3, *one), (16, 3, *one)],
        us=2,
        scratch=[pltpu.VMEM((2, *one), F32)],
    )
    x5s = [x5p] + [across_front(x5p, j) for j in (1, 2, 3)]
    (operand,) = call(
        level3_operand_kernel,
        "level3_operand",
        coords,
        [x4, mine, across(theirs, 1)],
        [(16, 4, *one)],
    )
    parts3 = swap16(operand)
    x3, x4p, mine, theirs = call(
        level3_back_kernel,
        "level3_back",
        coords,
        [parts3, y3, inverses, mats3],
        [one, (8, *one), (8, *one), (8, *one)],
        us=1.5,
        scratch=[pltpu.VMEM((16, *one), F32)],
    )
    x5m = pack(coords, x5s)
    x5o = across(x5m, 1)
    x4s = [x4p] + [across_front(x4p, j) for j in (1, 2, 3)]
    keep, message = call(
        pair_message_kernel,
        "pair_message",
        coords,
        [mine, across(theirs, 1), x3],
        [(4, *one), (5, *one)],
        after=x5s[1:],
    )
    (message,) = call(
        pair_sum_kernel, "pair_sum", coords, [keep, across(message, 6), x3], [(6, *one)]
    )
    (mine,) = call(
        pair_total_kernel,
        "pair_total",
        coords,
        [message, across(message, 2)],
        [(8, *one)],
        after=x4s[1:],
    )
    x1, x2, x123 = call(
        level12_back_kernel,
        "level12_back",
        coords,
        [mine, across(mine, 1), solved12, *group],
        [one, one, (14, *one)],
        us=2,
        scratch=[pltpu.VMEM((8, *one), F32)],
    )
    x4m = pack(coords, x4s)
    x4o = across(x4m, 1)
    rhs, couplings, items = leaf_high(
        coords, pattern, load_leaf, leaf_inverse, leaf_coupling, [x4m, x4o, x5m, x5o]
    )
    lows = [x123] + [across_front(x123, j) for j in (1, 2, 3)]
    solution_leaf = leaf_low(coords, pattern, items, lows, rhs, leaf_inverse, couplings)
    solution_sep = jnp.concatenate([x1, x2, x3, x4, x5], axis=1)
    return solution_leaf, solution_sep


def solution(mesh):
    return jax.shard_map(
        local,
        mesh=mesh,
        in_specs=(
            P(None, ("leaf", "front")),
            P(("leaf", "front"), None, None),
            P(("leaf", "front"), None, None, None),
            P(("leaf", "front"), None),
            P("front", "leaf"),
            P("leaf", None, None),
            P("leaf", None, None),
        ),
        out_specs=(P(None, ("leaf", "front")), P("front", "leaf")),
        check_vma=False,
    )
```

```python
import jax
import jax.numpy as jnp
from jax import lax
from jax.experimental import pallas as pl
from jax.experimental.pallas import tpu as pltpu
from jax.sharding import PartitionSpec as P

F32 = jnp.float32
BF16 = jnp.bfloat16
BLK = 128
COLS = 32
VMEM_BYTES = 32 * 1024 * 1024
LARGE_VMEM_BYTES = 48 * 1024 * 1024
RUNS = {(2, 1): 0, (3, 1): 4, (3, 2): 12, (4, 1): 20, (4, 2): 36, (4, 3): 52}
RUNS |= {(5, 1): 68, (5, 2): 100, (5, 3): 132, (5, 4): 164}
CHUNK = 8


def split(value):
    high = value.astype(BF16)
    low = (value - high.astype(F32)).astype(BF16)
    return high, low


def stacked(value):
    return jnp.concatenate(split(value), axis=0)


def beside(value):
    return jnp.concatenate(split(value), axis=1)


def dot_nt(left, right):
    return lax.dot_general(left, right, (((1,), (1,)), ((), ())), preferred_element_type=F32)


def dot_nn(left, right):
    return lax.dot_general(left, right, (((1,), (0,)), ((), ())), preferred_element_type=F32)


def fold(terms):
    rows = terms.shape[0] // 2
    return (terms[:rows, :BLK] + terms[:rows, BLK:]) + (terms[rows:, :BLK] + terms[rows:, BLK:])


def times_transposed(value, matrix):
    return fold(dot_nt(stacked(value), stacked(matrix)))


def times(value, matrix):
    return fold(dot_nn(stacked(value), beside(matrix)))


def sum_times_transposed(lefts, matrices):
    total = None
    for k in range(0, len(lefts), 2):
        left = jnp.concatenate([lefts[k], lefts[k + 1]], axis=1)
        right = jnp.concatenate([stacked(matrices[k]), stacked(matrices[k + 1])], axis=1)
        part = dot_nt(left, right)
        total = part if total is None else total + part
    return total


def wide_left(value):
    both = stacked(value)
    return jnp.concatenate([both, both], axis=1)


def two_times(left, first, second):
    right = jnp.concatenate([stacked(first), stacked(second)], axis=1)
    out = dot_nn(left, right)
    rows = out.shape[0] // 2
    out = out[:rows] + out[rows:]
    return out[:, :BLK], out[:, BLK:]


def cost(us):
    return pl.CostEstimate(
        flops=int(us * 1e9), bytes_accessed=int(us * 3e6), transcendentals=0
    )


def call(
    body, name, coords, inputs, outs, us=1.0, in_hbm=(), after=(), through=(), scratch=(), limit=VMEM_BYTES
):
    count, results = len(inputs), len(outs)
    extra = len(after) + len(through)

    def kernel(coords_ref, *refs):
        refs = list(refs)
        del refs[count + extra + results : count + extra + results + len(through)]
        del refs[count : count + extra]
        body(coords_ref, *refs)

    anywhere = pl.BlockSpec(memory_space=pl.ANY)
    hbm = pl.BlockSpec(memory_space=pltpu.HBM)
    vmem = pl.BlockSpec(memory_space=pltpu.VMEM)
    specs = [hbm if k in in_hbm else vmem for k in range(count)] + [anywhere] * extra
    first = 1 + count + len(after)
    return pl.pallas_call(
        kernel,
        name=name,
        out_shape=[jax.ShapeDtypeStruct(shape, F32) for shape in outs]
        + [jax.ShapeDtypeStruct(array.shape, array.dtype) for array in through],
        grid_spec=pltpu.PrefetchScalarGridSpec(
            num_scalar_prefetch=1,
            grid=(1,),
            in_specs=specs,
            out_specs=[vmem] * results + [anywhere] * len(through),
            scratch_shapes=list(scratch),
        ),
        input_output_aliases={first + k: results + k for k in range(len(through))},
        compiler_params=pltpu.CompilerParams(vmem_limit_bytes=limit),
        cost_estimate=cost(us),
    )(coords, *inputs, *after, *through)


def fetch(source, first, count, target, sems):
    for k in range(0, count, CHUNK):
        pltpu.make_async_copy(
            source.at[pl.ds(first + k, CHUNK)], target.at[pl.ds(k, CHUNK)], sems.at[k // CHUNK]
        ).start()


def fetched(source, first, target, sems, k):
    pltpu.make_async_copy(
        source.at[pl.ds(first + k * CHUNK, CHUNK)], target.at[pl.ds(k * CHUNK, CHUNK)], sems.at[k]
    ).wait()


def matrices(count):
    return [pltpu.VMEM((count, BLK, BLK), F32), pltpu.SemaphoreType.DMA((count // CHUNK,))]


PER_COPY = 2


def leaf_copies(load, inverse, coupling, loads, inverses, couplings, sems, blocks):
    copies = [
        pltpu.make_async_copy(load, loads, sems.at[0]),
        pltpu.make_async_copy(inverse, inverses, sems.at[1]),
    ]
    for k in range(blocks // PER_COPY):
        part = pl.ds(k * PER_COPY, PER_COPY)
        copies.append(
            pltpu.make_async_copy(coupling.at[part], couplings.at[part], sems.at[2 + k])
        )
    return copies


def leaf_forward_kernel(
    coords, pattern, load, inverse, coupling, load_sep,
    mine13, theirs13, mine45, theirs45,
    loads, inverses, couplings, load_seps, solved, sums, columns, sems, sep_sem,
):
    blocks = couplings.shape[0]
    core, y_at, x_at, front = coords[0], coords[1], coords[2], coords[3]
    copies = leaf_copies(load, inverse, coupling, loads, inverses, couplings, sems, blocks)
    sep_copy = pltpu.make_async_copy(load_sep, load_seps, sep_sem)
    sep_copy.start()
    for copy in copies:
        copy.start()
    sums[...] = jnp.zeros_like(sums)
    columns[...] = jnp.zeros_like(columns)
    rows = pl.ds(pl.multiple_of(front * COLS, COLS), COLS)
    slots = (
        core,
        2 + (y_at & 1) * 2 + core,
        6 + y_at,
        10 + (x_at & 1) * 4 + y_at,
        18 + x_at * 4 + y_at,
    )
    sep_copy.wait()
    for level, slot in enumerate(slots):
        columns[rows, :] = -load_seps[:, level * BLK : (level + 1) * BLK]
        sums[slot] = columns[...].T
    copies[0].wait()
    copies[1].wait()
    for b in range(blocks):
        turned = fold(
            dot_nt(stacked(inverses[b]), stacked(loads[:, b * BLK : (b + 1) * BLK]))
        )
        solved[b] = beside(turned)

    for k in range(blocks // PER_COPY):
        copies[2 + k].wait()
        for b in range(k * PER_COPY, (k + 1) * PER_COPY):
            right = jnp.concatenate([solved[b], solved[b]], axis=0)
            left = jnp.concatenate([beside(couplings[b, q]) for q in range(8)], axis=0)
            out = dot_nn(left, right)
            out = out[:, :BLK] + out[:, BLK:]
            for q in range(8):
                index = pattern[b, q]
                slot = jnp.where(index < 6, index, 6 + ((index - 6) >> 1))
                slot = jnp.where((index >= 6) & ((index & 1) != core), slot + 34, slot)
                sums[slot] += out[q * BLK : (q + 1) * BLK]

    mine13[...] = sums[0:10]
    theirs13[0:6] = sums[0:6]
    theirs13[6:10] = sums[40:44]
    mine45[...] = sums[10:34]
    theirs45[...] = sums[44:68]


def leaf_forward(coords, pattern, load_leaf, leaf_inverse, leaf_coupling, load_sep):
    blocks = leaf_inverse.shape[0]
    outs = [(10, BLK, BLK), (10, BLK, BLK), (24, BLK, BLK), (24, BLK, BLK)]
    vmem = pl.BlockSpec(memory_space=pltpu.VMEM)
    return pl.pallas_call(
        leaf_forward_kernel,
        name="leaf_forward",
        out_shape=[jax.ShapeDtypeStruct(shape, F32) for shape in outs],
        grid_spec=pltpu.PrefetchScalarGridSpec(
            num_scalar_prefetch=2,
            grid=(1,),
            in_specs=[pl.BlockSpec(memory_space=pltpu.HBM)] * 4,
            out_specs=[vmem] * 4,
            scratch_shapes=[
                pltpu.VMEM(load_leaf.shape, F32),
                pltpu.VMEM(leaf_inverse.shape, F32),
                pltpu.VMEM(leaf_coupling.shape, F32),
                pltpu.VMEM(load_sep.shape, F32),
                pltpu.VMEM((blocks, BLK, 2 * BLK), BF16),
                pltpu.VMEM((68, BLK, BLK), F32),
                pltpu.VMEM((BLK, BLK), F32),
                pltpu.SemaphoreType.DMA((2 + blocks // PER_COPY,)),
                pltpu.SemaphoreType.DMA,
            ],
        ),
        compiler_params=pltpu.CompilerParams(vmem_limit_bytes=LARGE_VMEM_BYTES),
        cost_estimate=cost(6),
    )(coords, pattern, load_leaf, leaf_inverse, leaf_coupling, load_sep)


def front_parts(coords, mine, received, cuts, through=(), after=()):
    def kernel(coords_ref, mine_ref, received_ref, *refs):
        outs, rows_of = refs[:-1], refs[-1]
        for k in range(mine.shape[0]):
            rows_of[k] = (mine_ref[k] + received_ref[k]).T
        for j in range(4):
            rows = pl.ds(pl.multiple_of((coords_ref[3] ^ j) * COLS, COLS), COLS)
            for c in range(len(cuts) - 1):
                outs[c * 4 + j][...] = rows_of[cuts[c] : cuts[c + 1], rows, :]

    counts = [cuts[c + 1] - cuts[c] for c in range(len(cuts) - 1)]
    return call(
        kernel,
        "front_parts",
        coords,
        [mine, received],
        [(count, COLS, BLK) for count in counts for _ in range(4)],
        after=after,
        through=through,
        scratch=[pltpu.VMEM(mine.shape, F32)],
    )


def preload(coords, sources, us=2.0, after=()):
    def kernel(coords_ref, *refs):
        count = len(sources)
        copies = []
        for k, (array, first, size) in enumerate(sources):
            part = refs[k].at[pl.ds(first, size)]
            copies.append(pltpu.make_async_copy(part, refs[count + k], refs[-1].at[k]))
            copies[-1].start()
        for copy in copies:
            copy.wait()

    return call(
        kernel,
        "preload",
        coords,
        [array for array, _, _ in sources],
        [(size, BLK, BLK) for _, _, size in sources],
        us=us,
        in_hbm=tuple(range(len(sources))),
        after=after,
        scratch=[pltpu.SemaphoreType.DMA((len(sources),))],
        limit=LARGE_VMEM_BYTES,
    )


def level12_message_kernel(coords, own, part1, part2, part3, keep, message):
    total = (own[...] + part1[...]) + (part2[...] + part3[...])
    y_at = coords[1]
    keep[0:6] = total[0:6]
    message[0:6] = total[0:6]

    def level3(j):
        row = pl.ds(6 + (y_at ^ j), 1)
        return (own[row] + part1[row]) + (part2[row] + part3[row])

    keep[6:7] = level3(0)
    keep[7:8] = level3(3)
    message[6:7] = level3(1)
    message[7:8] = level3(2)


def level12_kernel(
    coords, keep, received, own6, core6, y6, diagonal6, solved, message, left1, level1
):
    core, y_bit = coords[0], coords[1] & 1
    members = []
    for dy in range(2):
        for dc in range(2):
            members.append(((y_bit ^ dy) * 2 + (core ^ dc), dy, core ^ dc))
    mats = (own6, core6, y6, diagonal6)
    for (index, dy, at), mat in zip(members, mats):
        source = received if dy else keep
        here = times_transposed(-source[at], mat[0])
        solved[index] = here
        left1[index] = stacked(here)
    for (index, dy, at), mat in zip(members, mats):
        acc = sum_times_transposed([left1[m] for m in range(4)], [mat[2 + m] for m in range(4)])
        rhs = -(keep[2 + index] + received[2 + index]) - fold(acc)
        solved[4 + index] = times_transposed(rhs, mat[1])
    message[0:8] = solved[0:8]
    solved[8] = keep[6] + received[6]
    message[8] = keep[7] + received[7]


def level3_kernel(
    coords, solved, received, sums4, inverse, mats, y3, message, y12, y12p, left
):
    core, y_at, x_bit = coords[0], coords[1], coords[2] & 1
    half = y_at >> 1
    for level in range(2):
        for k in range(4):
            for source, part in ((solved, half), (received, 1 - half)):
                at = level * 8 + part * 4 + k
                y12[at] = source[level * 4 + k]
                left[at] = stacked(source[level * 4 + k])
    acc = sum_times_transposed([left[m] for m in range(16)], [mats[m] for m in range(16)])
    rhs = -(solved[8] + received[8]) - fold(acc)
    here = times_transposed(rhs, inverse[2])
    y3[...] = here
    message[0] = here
    message[1:5] = sums4[pl.ds((1 - x_bit) * 4, 4)]
    for level in range(2):
        for y in range(4):
            y12p[level * 4 + y] = y12[level * 8 + y * 2 + core]


def level4_sums_kernel(coords, own, part1, part2, part3, sums4):
    sums4[...] = (own[...] + part1[...]) + (part2[...] + part3[...])


def level4_pair_kernel(coords, y3, sums4, received, own, message1, message2, message3):
    y_at, x_bit = coords[1], coords[2] & 1
    for j, out in enumerate((own, message1, message2, message3)):
        row = y_at ^ j
        out[0] = y3[...]
        out[1] = received[0]
        out[2] = sums4[x_bit * 4 + row] + received[1 + row]


def level4_pack_kernel(coords, own, part1, part2, part3, r8, low16, total):
    y_at, x_bit = coords[1], coords[2] & 1
    for j, part in enumerate((own, part1, part2, part3)):
        low16[x_bit * 4 + (y_at ^ j)] = part[0]
        low16[(1 - x_bit) * 4 + (y_at ^ j)] = part[1]
    low16[8:16] = r8[...]
    total[...] = (own[2] + part1[2]) + (part2[2] + part3[2])


def level5_sums_kernel(coords, own, part1, part2, part3, sums5):
    sums5[...] = (own[...] + part1[...]) + (part2[...] + part3[...])


def half_lefts(left, core, line, mine, other, rest):
    for p in range(8):
        left[32 + 2 * p + core] = stacked(mine[p])
        left[32 + 2 * p + 1 - core] = stacked(other[p])
    for level in range(2):
        for y in range(4):
            at = level * 16 + line * 8 + 2 * y
            left[at + core] = stacked(mine[8 + level * 4 + y])
            left[at + 1 - core] = stacked(other[8 + level * 4 + y])
        rest(level, level * 16 + (1 - line) * 8)


def own_half_lefts(left, coords, low, other, y12):
    def rest(level, at):
        for m in range(8):
            left[at + m] = stacked(y12[level * 8 + m])

    half_lefts(left, coords[0], 1 - (coords[2] & 1), low, other, rest)


def level4_kernel(
    coords, low, other, y12, total, sums5, inverse, mats, y4, operand, left
):
    own_half_lefts(left, coords, low, other, y12)
    terms = sum_times_transposed([left[m] for m in range(48)], [mats[m] for m in range(48)])
    here = times_transposed(-total[...] - fold(terms), inverse[3])
    y4[...] = here
    for p in range(16):
        operand[p, 0] = here
        operand[p, 1] = sums5[p]


def fetch_half(coupling, half, target, sems):
    copies = []
    for level in range(3):
        source = coupling.at[pl.ds(RUNS[5, 1] + level * 32 + half * 16, 16)]
        copies.append(
            pltpu.make_async_copy(source, target.at[pl.ds(level * 16, 16)], sems.at[level])
        )
        copies[-1].start()
    return copies


def half_products(copies, left, mats):
    total = None
    for level, copy in enumerate(copies):
        copy.wait()
        rows = range(level * 16, level * 16 + 16)
        part = sum_times_transposed([left[m] for m in rows], [mats[m] for m in rows])
        total = part if total is None else total + part
    return total


def level5_own_kernel(coords, low, other, y12, coupling, acc, mats, sems, left):
    copies = fetch_half(coupling, coords[2] >> 1, mats, sems)
    own_half_lefts(left, coords, low, other, y12)
    acc[...] = half_products(copies, left, mats)


def level5_far_kernel(
    coords, low, other, line, line_other, own, coupling, acc, mats54, mats, sems, left, sem
):
    copies = fetch_half(coupling, 1 - (coords[2] >> 1), mats, sems)
    last = pltpu.make_async_copy(coupling.at[pl.ds(RUNS[5, 4], 32)], mats54, sem)
    last.start()
    core = coords[0]

    def rest(level, at):
        for y in range(4):
            left[at + 2 * y + core] = stacked(line[level * 4 + y])
            left[at + 2 * y + 1 - core] = stacked(line_other[level * 4 + y])

    half_lefts(left, core, coords[2] & 1, low, other, rest)
    acc[...] = own[...] + half_products(copies, left, mats)
    last.wait()


def level5_kernel(coords, acc, mine, other, inverse, mats, x5, own, theirs, left, pair):
    core = coords[0]
    total = mine[0, 1]
    for p in range(1, 16):
        total = total + mine[p, 1]
    for p in range(16):
        left[p * 2 + core] = stacked(mine[p, 0])
        left[p * 2 + 1 - core] = stacked(other[p, 0])
    terms = acc[...] + sum_times_transposed(
        [left[m] for m in range(32)], [mats[m] for m in range(32)]
    )
    solved = times_transposed(-total - fold(terms), inverse[4])
    here = times(solved, inverse[4])
    x5[...] = here
    wide = wide_left(here)
    for p in range(16):
        pair[2 * p], pair[2 * p + 1] = two_times(wide, mats[2 * p], mats[2 * p + 1])
    for p in range(16):
        own[p] = pair[2 * p + core]
        theirs[p] = pair[2 * p + 1 - core]


def level4_operand_kernel(coords, x5, own, received, operand):
    for p in range(16):
        operand[p, 0] = own[p] + received[p]
        operand[p, 1] = x5[...]


def level5_back_kernel(coords, x5, coupling, spread, mats4, mats, sems, sem):
    fetch(coupling, RUNS[5, 1], 96, mats, sems)
    last = pltpu.make_async_copy(coupling.at[pl.ds(RUNS[4, 1], 48)], mats4, sem)
    last.start()
    wide = wide_left(x5[...])

    def step(i, _):
        fetched(coupling, RUNS[5, 1], mats, sems, i)
        for k in range(0, CHUNK, 2):
            at = i * CHUNK + k
            spread[at], spread[at + 1] = two_times(wide, mats[at], mats[at + 1])
        return 0

    lax.fori_loop(0, 96 // CHUNK, step, 0)
    last.wait()


def level4_back_kernel(coords, parts, y4, spread, inverse, mats, x4, x5p, mine, theirs, all4):
    core, half = coords[0], coords[2] >> 1
    total = parts[0, 0]
    for p in range(1, 16):
        total = total + parts[p, 0]
    for p in range(16):
        x5p[p] = parts[p, 1]
    here = times(y4[...] - total, inverse[3])
    x4[...] = here
    wide = wide_left(here)
    for level in range(3):
        for pair in range(16):
            mine[pair, level] = spread[level * 32 + pair * 2 + core]
            theirs[pair, level] = spread[level * 32 + pair * 2 + 1 - core]
        for pair in range(8):
            at = level * 16 + pair * 2
            all4[0], all4[1] = two_times(wide, mats[at], mats[at + 1])
            mine[half * 8 + pair, level] += all4[core]
            theirs[half * 8 + pair, level] += all4[1 - core]


def level3_operand_kernel(coords, x4, mine, received, operand):
    for p in range(16):
        operand[p, 0:3] = mine[p] + received[p]
        operand[p, 3] = x4[...]


def level3_back_kernel(coords, parts, y3, inverse, mats, x3, x4p, mine, theirs, spread):
    core, y_at = coords[0], coords[1]
    sums = []
    for level in range(3):
        total = parts[0, level]
        for p in range(1, 16):
            total = total + parts[p, level]
        sums.append(total)
    for p in range(8):
        x4p[p] = parts[(coords[2] >> 1) * 8 + p, 3]
    here = times(y3[...] - sums[2], inverse[2])
    x3[...] = here
    wide = wide_left(here)
    for pair in range(8):
        spread[2 * pair], spread[2 * pair + 1] = two_times(wide, mats[2 * pair], mats[2 * pair + 1])
    for level in range(2):
        spread[level * 8 + y_at * 2 + core] += sums[level]
    for pair in range(8):
        mine[pair] = spread[2 * pair + core]
        theirs[pair] = spread[2 * pair + 1 - core]


def pair_message_kernel(coords, mine, received, x3, keep, message):
    half = coords[1] >> 1
    for level in range(2):
        for out, part in ((keep, half), (message, 1 - half)):
            rows = pl.ds(level * 4 + part * 2, 2)
            out[level * 2 : level * 2 + 2] = mine[rows] + received[rows]
    message[4] = x3[...]


def pair_sum_kernel(coords, keep, received, x3, message):
    message[0:4] = keep[...] + received[0:4]
    message[4] = x3[...]
    message[5] = received[4]


def pair_total_kernel(coords, message, received, out):
    out[0:4] = message[0:4] + received[0:4]
    out[4:6] = message[4:6]
    out[6:8] = received[4:6]


def level12_back_kernel(
    coords, mine, other, solved, own6, core6, y6, diagonal6, own1, own2, x123, terms
):
    core, y_at = coords[0], coords[1]
    y_bit = y_at & 1
    for source, parity in ((mine, core), (other, 1 - core)):
        for level in range(2):
            for y in range(2):
                terms[level * 4 + y * 2 + parity] = source[level * 2 + y]
        for k, dy in enumerate((0, 3, 1, 2)):
            x123[6 + (y_at ^ dy) * 2 + parity] = source[4 + k]
    members = [
        ((y_bit ^ dy) * 2 + (core ^ dc), dy, core ^ dc) for dy in range(2) for dc in range(2)
    ]
    mats = (own6, core6, y6, diagonal6)
    for k, ((index, dy, at), mat) in enumerate(zip(members, mats)):
        here = times(solved[4 + index] - terms[4 + index], mat[1])
        x123[2 + index] = here
        if k == 0:
            own2[...] = here
        wide = wide_left(here)
        for m in range(0, 4, 2):
            first, second = two_times(wide, mat[2 + m], mat[3 + m])
            terms[m] += first
            terms[m + 1] += second
    for k in range(2):
        index, dy, at = members[k]
        here = times(solved[index] - terms[index], mats[k][0])
        x123[at] = here
        if k == 0:
            own1[...] = here


LOW = 14
AT_ONCE = 4


def pack_kernel(coords, part0, part1, part2, part3, out):
    for j, part in enumerate((part0, part1, part2, part3)):
        out[j] = part[...]


def pack(coords, parts):
    return call(pack_kernel, "pack", coords, parts, [(4, *parts[0].shape)])[0]


def place(blocks, index, front, j, value):
    high, low = split(value)
    at = pl.multiple_of((front ^ j) * COLS, COLS)
    blocks[index, pl.ds(at, COLS), :] = high
    blocks[index, pl.ds(BLK + at, COLS), :] = low


def leaf_high_kernel(
    coords, pattern, load, inverse, coupling, x4m, x4o, x5m, x5o,
    rhs, couplings, items,
    loads, inverses, blocks, sems,
):
    count = couplings.shape[0]
    core, front = coords[0], coords[3]
    copies = leaf_copies(load, inverse, coupling, loads, inverses, couplings, sems, count)
    for copy in copies:
        copy.start()

    def note(i, found):
        items[1 + found] = i
        return found + (pattern[i >> 3, i & 7] < LOW).astype(jnp.int32)

    items[0] = lax.fori_loop(0, count * 8, note, jnp.int32(0))
    blocks[48] = jnp.zeros((2 * BLK, BLK), BF16)
    for j in range(4):
        for p in range(8):
            place(blocks, 2 * p + core, front, j, x4m[j, p])
            place(blocks, 2 * p + 1 - core, front, j, x4o[j, p])
        for p in range(16):
            place(blocks, 16 + 2 * p + core, front, j, x5m[j, p])
            place(blocks, 16 + 2 * p + 1 - core, front, j, x5o[j, p])
    copies[0].wait()
    copies[1].wait()
    for k in range(count // PER_COPY):
        copies[2 + k].wait()
        for b in range(k * PER_COPY, (k + 1) * PER_COPY):
            here = times_transposed(loads[:, b * BLK : (b + 1) * BLK], inverses[b])
            total = None
            for q in range(0, 8, 2):
                indices = [pattern[b, q + k2] for k2 in range(2)]
                chosen = [jnp.where(index < LOW, 48, index - LOW) for index in indices]
                left = jnp.concatenate([blocks[c] for c in chosen], axis=1)
                right = jnp.concatenate([beside(couplings[b, q + k2]) for k2 in range(2)], axis=0)
                part = dot_nn(left, right)
                total = part if total is None else total + part
            rhs[b] = here - fold(total)


def leaf_high(coords, pattern, load_leaf, leaf_inverse, leaf_coupling, gathered):
    blocks = leaf_inverse.shape[0]
    vmem = pl.BlockSpec(memory_space=pltpu.VMEM)
    return pl.pallas_call(
        leaf_high_kernel,
        name="leaf_high",
        out_shape=[
            jax.ShapeDtypeStruct((blocks, BLK, BLK), F32),
            jax.ShapeDtypeStruct(leaf_coupling.shape, F32),
            jax.ShapeDtypeStruct((blocks * 8 + 2,), jnp.int32),
        ],
        grid_spec=pltpu.PrefetchScalarGridSpec(
            num_scalar_prefetch=2,
            grid=(1,),
            in_specs=[pl.BlockSpec(memory_space=pltpu.HBM)] * 3 + [vmem] * 4,
            out_specs=[vmem, vmem, pl.BlockSpec(memory_space=pltpu.SMEM)],
            scratch_shapes=[
                pltpu.VMEM(load_leaf.shape, F32),
                pltpu.VMEM(leaf_inverse.shape, F32),
                pltpu.VMEM((49, 2 * BLK, BLK), BF16),
                pltpu.SemaphoreType.DMA((2 + blocks // PER_COPY,)),
            ],
        ),
        compiler_params=pltpu.CompilerParams(vmem_limit_bytes=VMEM_BYTES),
        cost_estimate=cost(8),
    )(coords, pattern, load_leaf, leaf_inverse, leaf_coupling, *gathered)


def leaf_low_kernel(
    coords, pattern, items, low0, low1, low2, low3, rhs, inverse, couplings,
    out,
    blocks, acc, solved, sems,
):
    front, count = coords[3], items[0]
    acc[...] = rhs[...]
    blocks[LOW] = jnp.zeros((2 * BLK, BLK), BF16)
    for j, low in enumerate((low0, low1, low2, low3)):
        for a in range(LOW):
            place(blocks, a, front, j, low[a])

    def step(t, _):
        for k in range(AT_ONCE):
            at = t * AT_ONCE + k
            item = jnp.where(at < count, items[1 + jnp.minimum(at, count)], 0)
            index = jnp.where(at < count, pattern[item >> 3, item & 7], LOW)
            right = beside(couplings[item >> 3, item & 7])
            acc[item >> 3] -= fold(dot_nn(blocks[index], right))
        return 0

    lax.fori_loop(0, (count + AT_ONCE - 1) // AT_ONCE, step, 0)
    copies = []
    for b in range(rhs.shape[0]):
        solved[b] = times(acc[b], inverse[b])
        copies.append(
            pltpu.make_async_copy(solved.at[b], out.at[:, b * BLK : (b + 1) * BLK], sems.at[b])
        )
        copies[-1].start()
    for copy in copies:
        copy.wait()


def leaf_low(coords, pattern, items, lows, rhs, leaf_inverse, couplings):
    blocks = leaf_inverse.shape[0]
    vmem = pl.BlockSpec(memory_space=pltpu.VMEM)
    return pl.pallas_call(
        leaf_low_kernel,
        name="leaf_low",
        out_shape=jax.ShapeDtypeStruct((BLK, blocks * BLK), F32),
        grid_spec=pltpu.PrefetchScalarGridSpec(
            num_scalar_prefetch=3,
            grid=(1,),
            in_specs=[vmem] * 7,
            out_specs=pl.BlockSpec(memory_space=pltpu.HBM),
            scratch_shapes=[
                pltpu.VMEM((LOW + 1, 2 * BLK, BLK), BF16),
                pltpu.VMEM((blocks, BLK, BLK), F32),
                pltpu.VMEM((blocks, BLK, BLK), F32),
                pltpu.SemaphoreType.DMA((blocks,)),
            ],
        ),
        compiler_params=pltpu.CompilerParams(vmem_limit_bytes=VMEM_BYTES),
        cost_estimate=cost(4),
    )(coords, pattern, items, *lows, rhs, leaf_inverse, couplings)


def across(value, mask):
    return lax.ppermute(value, "leaf", [(i, i ^ mask) for i in range(32)])


def across_front(value, mask):
    return lax.ppermute(value, "front", [(i, i ^ mask) for i in range(4)])


def swap16(value):
    groups = [[c + 2 * p for p in range(16)] for c in (0, 1)]
    return lax.all_to_all(value, "leaf", 0, 0, axis_index_groups=groups)


def local(
    load_leaf, leaf_inverse, leaf_coupling, leaf_pattern, load_sep, sep_inverse, sep_coupling
):
    leaf_at = lax.axis_index("leaf")
    coords = jnp.stack([leaf_at & 1, (leaf_at >> 1) & 3, leaf_at >> 3, lax.axis_index("front")])
    coords = coords.astype(jnp.int32)
    pattern = leaf_pattern
    one = (COLS, BLK)
    wide = (2 * COLS, 2 * BLK)
    left = lambda count: pltpu.VMEM((count, 2 * COLS, BLK), BF16)
    own6 = jnp.concatenate([sep_inverse[0:2], sep_coupling[0:4]], axis=0)
    mine13, theirs13, mine45, theirs45 = leaf_forward(
        coords, pattern, load_leaf, leaf_inverse, leaf_coupling, load_sep
    )
    *parts13, theirs45, own6 = front_parts(
        coords, mine13, across(theirs13, 1), (0, 10), through=[theirs45, own6]
    )
    parts13 = [parts13[0]] + [across_front(parts13[j], j) for j in (1, 2, 3)]
    y6 = across(own6, 2)
    core6 = across(own6, 1)
    parts45 = front_parts(coords, mine45, across(theirs45, 1), (0, 8, 24))
    parts4, parts5 = parts45[0:4], parts45[4:8]
    inverses, mats3, mats4 = preload(
        coords,
        [(sep_inverse, 0, 5), (sep_coupling, RUNS[3, 1], 16), (sep_coupling, RUNS[4, 1], 48)],
        after=[parts45[0]],
    )
    keep, message, y6 = call(
        level12_message_kernel,
        "level12_message",
        coords,
        parts13,
        [(8, *one), (8, *one)],
        after=[parts45[0], mats3],
        through=[y6],
    )
    diagonal6 = across(y6, 1)
    group = [own6, core6, y6, diagonal6]
    parts4 = [parts4[0]] + [across_front(parts4[j], j) for j in (1, 2, 3)]
    solved12, message = call(
        level12_kernel,
        "level12",
        coords,
        [keep, across(message, 2), *group],
        [(9, *one), (9, *one)],
        us=2,
        scratch=[left(4), pltpu.VMEM((8, 128), F32)],
    )
    (sums4,) = call(
        level4_sums_kernel, "level4_sums", coords, parts4, [(8, *one)]
    )
    parts5 = [parts5[0]] + [across_front(parts5[j], j) for j in (1, 2, 3)]
    y3, message, y12, y12p = call(
        level3_kernel,
        "level3",
        coords,
        [solved12, across(message, 6), sums4, inverses, mats3],
        [one, (5, *one), (16, *one), (8, *one)],
        us=2,
        scratch=[left(16)],
    )
    (sums5,) = call(level5_sums_kernel, "level5_sums", coords, parts5, [(16, *one)])
    r8 = across(y12p, 8)
    own, *messages = call(
        level4_pair_kernel,
        "level4_pair",
        coords,
        [y3, sums4, across(message, 8)],
        [(3, *one)] * 4,
    )
    parts = [own] + [across(messages[j - 1], 2 * j) for j in (1, 2, 3)]
    low16, total4 = call(
        level4_pack_kernel,
        "level4_pack",
        coords,
        [*parts, r8],
        [(16, *one), one],
        after=[sums5],
    )
    other16 = across(low16, 1)
    far16 = across(low16, 24)
    line8 = across(y12p, 24)
    line_other8 = across(line8, 1)
    y4, operand = call(
        level4_kernel,
        "level4",
        coords,
        [low16, other16, y12, total4, sums5, inverses, mats4],
        [one, (16, 2, *one)],
        us=3,
        scratch=[left(48)],
    )
    y4m = swap16(operand)
    far_other16 = across(far16, 1)
    (own5,) = call(
        level5_own_kernel,
        "level5_own",
        coords,
        [low16, other16, y12, sep_coupling],
        [wide],
        us=4,
        in_hbm=(3,),
        scratch=[pltpu.VMEM((48, BLK, BLK), F32), pltpu.SemaphoreType.DMA((3,)), left(48)],
        limit=LARGE_VMEM_BYTES,
    )
    acc5, mats54 = call(
        level5_far_kernel,
        "level5_far",
        coords,
        [far16, far_other16, line8, line_other8, own5, sep_coupling],
        [wide, (32, BLK, BLK)],
        us=4,
        in_hbm=(5,),
        scratch=[
            pltpu.VMEM((48, BLK, BLK), F32),
            pltpu.SemaphoreType.DMA((3,)),
            left(48),
            pltpu.SemaphoreType.DMA,
        ],
        limit=LARGE_VMEM_BYTES,
    )
    y4m, acc5, mats54 = lax.optimization_barrier((y4m, acc5, mats54))
    y4o = across(y4m, 1)
    x5, own4, theirs4 = call(
        level5_kernel,
        "level5",
        coords,
        [acc5, y4m, y4o, inverses, mats54],
        [one, (16, *one), (16, *one)],
        us=4,
        scratch=[left(32), pltpu.VMEM((32, *one), F32)],
    )
    (operand,) = call(
        level4_operand_kernel,
        "level4_operand",
        coords,
        [x5, own4, across(theirs4, 1)],
        [(16, 2, *one)],
    )
    sums4 = swap16(operand)
    spread, mats4 = call(
        level5_back_kernel,
        "level5_back",
        coords,
        [x5, sep_coupling],
        [(96, *one), (48, BLK, BLK)],
        us=6,
        in_hbm=(1,),
        scratch=[*matrices(96), pltpu.SemaphoreType.DMA],
        limit=LARGE_VMEM_BYTES,
    )
    x4, x5p, mine, theirs = call(
        level4_back_kernel,
        "level4_back",
        coords,
        [sums4, y4, spread, inverses, mats4],
        [one, (16, *one), (16, 3, *one), (16, 3, *one)],
        us=2,
        scratch=[pltpu.VMEM((2, *one), F32)],
    )
    x5s = [x5p] + [across_front(x5p, j) for j in (1, 2, 3)]
    (operand,) = call(
        level3_operand_kernel,
        "level3_operand",
        coords,
        [x4, mine, across(theirs, 1)],
        [(16, 4, *one)],
    )
    parts3 = swap16(operand)
    x3, x4p, mine, theirs = call(
        level3_back_kernel,
        "level3_back",
        coords,
        [parts3, y3, inverses, mats3],
        [one, (8, *one), (8, *one), (8, *one)],
        us=1.5,
        scratch=[pltpu.VMEM((16, *one), F32)],
    )
    x5m = pack(coords, x5s)
    x5o = across(x5m, 1)
    x4s = [x4p] + [across_front(x4p, j) for j in (1, 2, 3)]
    keep, message = call(
        pair_message_kernel,
        "pair_message",
        coords,
        [mine, across(theirs, 1), x3],
        [(4, *one), (5, *one)],
        after=x5s[1:],
    )
    (message,) = call(
        pair_sum_kernel, "pair_sum", coords, [keep, across(message, 6), x3], [(6, *one)]
    )
    (mine,) = call(
        pair_total_kernel,
        "pair_total",
        coords,
        [message, across(message, 2)],
        [(8, *one)],
        after=x4s[1:],
    )
    x1, x2, x123 = call(
        level12_back_kernel,
        "level12_back",
        coords,
        [mine, across(mine, 1), solved12, *group],
        [one, one, (14, *one)],
        us=2,
        scratch=[pltpu.VMEM((8, *one), F32)],
    )
    x4m = pack(coords, x4s)
    x4o = across(x4m, 1)
    rhs, couplings, items = leaf_high(
        coords, pattern, load_leaf, leaf_inverse, leaf_coupling, [x4m, x4o, x5m, x5o]
    )
    lows = [x123] + [across_front(x123, j) for j in (1, 2, 3)]
    solution_leaf = leaf_low(coords, pattern, items, lows, rhs, leaf_inverse, couplings)
    solution_sep = jnp.concatenate([x1, x2, x3, x4, x5], axis=1)
    return solution_leaf, solution_sep


def solution(mesh):
    return jax.shard_map(
        local,
        mesh=mesh,
        in_specs=(
            P(None, ("leaf", "front")),
            P(("leaf", "front"), None, None),
            P(("leaf", "front"), None, None, None),
            P(("leaf", "front"), None),
            P("front", "leaf"),
            P("leaf", None, None),
            P("leaf", None, None),
        ),
        out_specs=(P(None, ("leaf", "front")), P("front", "leaf")),
        check_vma=False,
    )
```

```python
import jax
import jax.numpy as jnp
from jax import lax
from jax.experimental import pallas as pl
from jax.experimental.pallas import tpu as pltpu
from jax.sharding import PartitionSpec as P

F32 = jnp.float32
BF16 = jnp.bfloat16
BLK = 128
COLS = 32
VMEM_BYTES = 32 * 1024 * 1024
LARGE_VMEM_BYTES = 48 * 1024 * 1024
RUNS = {(2, 1): 0, (3, 1): 4, (3, 2): 12, (4, 1): 20, (4, 2): 36, (4, 3): 52}
RUNS |= {(5, 1): 68, (5, 2): 100, (5, 3): 132, (5, 4): 164}
CHUNK = 8


def split(value):
    high = value.astype(BF16)
    low = (value - high.astype(F32)).astype(BF16)
    return high, low


def stacked(value):
    return jnp.concatenate(split(value), axis=0)


def beside(value):
    return jnp.concatenate(split(value), axis=1)


def dot_nt(left, right):
    return lax.dot_general(left, right, (((1,), (1,)), ((), ())), preferred_element_type=F32)


def dot_nn(left, right):
    return lax.dot_general(left, right, (((1,), (0,)), ((), ())), preferred_element_type=F32)


def fold(terms):
    rows = terms.shape[0] // 2
    return (terms[:rows, :BLK] + terms[:rows, BLK:]) + (terms[rows:, :BLK] + terms[rows:, BLK:])


def times_transposed(value, matrix):
    return fold(dot_nt(stacked(value), stacked(matrix)))


def times(value, matrix):
    return fold(dot_nn(stacked(value), beside(matrix)))


def sum_times_transposed(lefts, matrices):
    total = None
    for k in range(0, len(lefts), 2):
        left = jnp.concatenate([lefts[k], lefts[k + 1]], axis=1)
        right = jnp.concatenate([stacked(matrices[k]), stacked(matrices[k + 1])], axis=1)
        part = dot_nt(left, right)
        total = part if total is None else total + part
    return total


def wide_left(value):
    both = stacked(value)
    return jnp.concatenate([both, both], axis=1)


def two_times(left, first, second):
    right = jnp.concatenate([stacked(first), stacked(second)], axis=1)
    out = dot_nn(left, right)
    rows = out.shape[0] // 2
    out = out[:rows] + out[rows:]
    return out[:, :BLK], out[:, BLK:]


def cost(us):
    return pl.CostEstimate(
        flops=int(us * 3e8), bytes_accessed=int(us * 1e6), transcendentals=0
    )


def call(
    body, name, coords, inputs, outs, us=1.0, in_hbm=(), after=(), through=(), scratch=(), limit=VMEM_BYTES
):
    count, results = len(inputs), len(outs)
    extra = len(after) + len(through)

    def kernel(coords_ref, *refs):
        refs = list(refs)
        del refs[count + extra + results : count + extra + results + len(through)]
        del refs[count : count + extra]
        body(coords_ref, *refs)

    anywhere = pl.BlockSpec(memory_space=pl.ANY)
    hbm = pl.BlockSpec(memory_space=pltpu.HBM)
    vmem = pl.BlockSpec(memory_space=pltpu.VMEM)
    specs = [hbm if k in in_hbm else vmem for k in range(count)] + [anywhere] * extra
    first = 1 + count + len(after)
    return pl.pallas_call(
        kernel,
        name=name,
        out_shape=[jax.ShapeDtypeStruct(shape, F32) for shape in outs]
        + [jax.ShapeDtypeStruct(array.shape, array.dtype) for array in through],
        grid_spec=pltpu.PrefetchScalarGridSpec(
            num_scalar_prefetch=1,
            grid=(1,),
            in_specs=specs,
            out_specs=[vmem] * results + [anywhere] * len(through),
            scratch_shapes=list(scratch),
        ),
        input_output_aliases={first + k: results + k for k in range(len(through))},
        compiler_params=pltpu.CompilerParams(vmem_limit_bytes=limit),
        cost_estimate=cost(us),
    )(coords, *inputs, *after, *through)


def fetch(source, first, count, target, sems):
    for k in range(0, count, CHUNK):
        pltpu.make_async_copy(
            source.at[pl.ds(first + k, CHUNK)], target.at[pl.ds(k, CHUNK)], sems.at[k // CHUNK]
        ).start()


def fetched(source, first, target, sems, k):
    pltpu.make_async_copy(
        source.at[pl.ds(first + k * CHUNK, CHUNK)], target.at[pl.ds(k * CHUNK, CHUNK)], sems.at[k]
    ).wait()


def matrices(count):
    return [pltpu.VMEM((count, BLK, BLK), F32), pltpu.SemaphoreType.DMA((count // CHUNK,))]


PER_COPY = 2


def leaf_copies(load, inverse, coupling, loads, inverses, couplings, sems, blocks):
    copies = [
        pltpu.make_async_copy(load, loads, sems.at[0]),
        pltpu.make_async_copy(inverse, inverses, sems.at[1]),
    ]
    for k in range(blocks // PER_COPY):
        part = pl.ds(k * PER_COPY, PER_COPY)
        copies.append(
            pltpu.make_async_copy(coupling.at[part], couplings.at[part], sems.at[2 + k])
        )
    return copies


def leaf_forward_kernel(
    coords, pattern, load, inverse, coupling, load_sep,
    mine13, theirs13, mine45, theirs45,
    loads, inverses, couplings, load_seps, solved, sums, columns, sems, sep_sem,
):
    blocks = couplings.shape[0]
    core, y_at, x_at, front = coords[0], coords[1], coords[2], coords[3]
    copies = leaf_copies(load, inverse, coupling, loads, inverses, couplings, sems, blocks)
    sep_copy = pltpu.make_async_copy(load_sep, load_seps, sep_sem)
    sep_copy.start()
    for copy in copies:
        copy.start()
    sums[...] = jnp.zeros_like(sums)
    columns[...] = jnp.zeros_like(columns)
    rows = pl.ds(pl.multiple_of(front * COLS, COLS), COLS)
    slots = (
        core,
        2 + (y_at & 1) * 2 + core,
        6 + y_at,
        10 + (x_at & 1) * 4 + y_at,
        18 + x_at * 4 + y_at,
    )
    sep_copy.wait()
    for level, slot in enumerate(slots):
        columns[rows, :] = -load_seps[:, level * BLK : (level + 1) * BLK]
        sums[slot] = columns[...].T
    copies[0].wait()
    copies[1].wait()
    for b in range(blocks):
        turned = fold(
            dot_nt(stacked(inverses[b]), stacked(loads[:, b * BLK : (b + 1) * BLK]))
        )
        solved[b] = beside(turned)

    for k in range(blocks // PER_COPY):
        copies[2 + k].wait()
        for b in range(k * PER_COPY, (k + 1) * PER_COPY):
            right = jnp.concatenate([solved[b], solved[b]], axis=0)
            left = jnp.concatenate([beside(couplings[b, q]) for q in range(8)], axis=0)
            out = dot_nn(left, right)
            out = out[:, :BLK] + out[:, BLK:]
            for q in range(8):
                index = pattern[b, q]
                slot = jnp.where(index < 6, index, 6 + ((index - 6) >> 1))
                slot = jnp.where((index >= 6) & ((index & 1) != core), slot + 34, slot)
                sums[slot] += out[q * BLK : (q + 1) * BLK]

    mine13[...] = sums[0:10]
    theirs13[0:6] = sums[0:6]
    theirs13[6:10] = sums[40:44]
    mine45[...] = sums[10:34]
    theirs45[...] = sums[44:68]


def leaf_forward(coords, pattern, load_leaf, leaf_inverse, leaf_coupling, load_sep):
    blocks = leaf_inverse.shape[0]
    outs = [(10, BLK, BLK), (10, BLK, BLK), (24, BLK, BLK), (24, BLK, BLK)]
    vmem = pl.BlockSpec(memory_space=pltpu.VMEM)
    return pl.pallas_call(
        leaf_forward_kernel,
        name="leaf_forward",
        out_shape=[jax.ShapeDtypeStruct(shape, F32) for shape in outs],
        grid_spec=pltpu.PrefetchScalarGridSpec(
            num_scalar_prefetch=2,
            grid=(1,),
            in_specs=[pl.BlockSpec(memory_space=pltpu.HBM)] * 4,
            out_specs=[vmem] * 4,
            scratch_shapes=[
                pltpu.VMEM(load_leaf.shape, F32),
                pltpu.VMEM(leaf_inverse.shape, F32),
                pltpu.VMEM(leaf_coupling.shape, F32),
                pltpu.VMEM(load_sep.shape, F32),
                pltpu.VMEM((blocks, BLK, 2 * BLK), BF16),
                pltpu.VMEM((68, BLK, BLK), F32),
                pltpu.VMEM((BLK, BLK), F32),
                pltpu.SemaphoreType.DMA((2 + blocks // PER_COPY,)),
                pltpu.SemaphoreType.DMA,
            ],
        ),
        compiler_params=pltpu.CompilerParams(vmem_limit_bytes=LARGE_VMEM_BYTES),
        cost_estimate=cost(6),
    )(coords, pattern, load_leaf, leaf_inverse, leaf_coupling, load_sep)


def front_parts(coords, mine, received, cuts, through=(), after=()):
    def kernel(coords_ref, mine_ref, received_ref, *refs):
        outs, rows_of = refs[:-1], refs[-1]
        for k in range(mine.shape[0]):
            rows_of[k] = (mine_ref[k] + received_ref[k]).T
        for j in range(4):
            rows = pl.ds(pl.multiple_of((coords_ref[3] ^ j) * COLS, COLS), COLS)
            for c in range(len(cuts) - 1):
                outs[c * 4 + j][...] = rows_of[cuts[c] : cuts[c + 1], rows, :]

    counts = [cuts[c + 1] - cuts[c] for c in range(len(cuts) - 1)]
    return call(
        kernel,
        "front_parts",
        coords,
        [mine, received],
        [(count, COLS, BLK) for count in counts for _ in range(4)],
        after=after,
        through=through,
        scratch=[pltpu.VMEM(mine.shape, F32)],
    )


def preload(coords, sources, us=2.0, after=()):
    def kernel(coords_ref, *refs):
        count = len(sources)
        copies = []
        for k, (array, first, size) in enumerate(sources):
            part = refs[k].at[pl.ds(first, size)]
            copies.append(pltpu.make_async_copy(part, refs[count + k], refs[-1].at[k]))
            copies[-1].start()
        for copy in copies:
            copy.wait()

    return call(
        kernel,
        "preload",
        coords,
        [array for array, _, _ in sources],
        [(size, BLK, BLK) for _, _, size in sources],
        us=us,
        in_hbm=tuple(range(len(sources))),
        after=after,
        scratch=[pltpu.SemaphoreType.DMA((len(sources),))],
        limit=LARGE_VMEM_BYTES,
    )


def level12_message_kernel(coords, own, part1, part2, part3, keep, message):
    total = (own[...] + part1[...]) + (part2[...] + part3[...])
    y_at = coords[1]
    keep[0:6] = total[0:6]
    message[0:6] = total[0:6]

    def level3(j):
        row = pl.ds(6 + (y_at ^ j), 1)
        return (own[row] + part1[row]) + (part2[row] + part3[row])

    keep[6:7] = level3(0)
    keep[7:8] = level3(3)
    message[6:7] = level3(1)
    message[7:8] = level3(2)


def level12_kernel(
    coords, keep, received, own6, core6, y6, diagonal6, solved, message, left1, level1
):
    core, y_bit = coords[0], coords[1] & 1
    members = []
    for dy in range(2):
        for dc in range(2):
            members.append(((y_bit ^ dy) * 2 + (core ^ dc), dy, core ^ dc))
    mats = (own6, core6, y6, diagonal6)
    for (index, dy, at), mat in zip(members, mats):
        source = received if dy else keep
        here = times_transposed(-source[at], mat[0])
        solved[index] = here
        left1[index] = stacked(here)
    for (index, dy, at), mat in zip(members, mats):
        acc = sum_times_transposed([left1[m] for m in range(4)], [mat[2 + m] for m in range(4)])
        rhs = -(keep[2 + index] + received[2 + index]) - fold(acc)
        solved[4 + index] = times_transposed(rhs, mat[1])
    message[0:8] = solved[0:8]
    solved[8] = keep[6] + received[6]
    message[8] = keep[7] + received[7]


def level3_kernel(
    coords, solved, received, sums4, inverse, mats, y3, message, y12, y12p, left
):
    core, y_at, x_bit = coords[0], coords[1], coords[2] & 1
    half = y_at >> 1
    for level in range(2):
        for k in range(4):
            for source, part in ((solved, half), (received, 1 - half)):
                at = level * 8 + part * 4 + k
                y12[at] = source[level * 4 + k]
                left[at] = stacked(source[level * 4 + k])
    acc = sum_times_transposed([left[m] for m in range(16)], [mats[m] for m in range(16)])
    rhs = -(solved[8] + received[8]) - fold(acc)
    here = times_transposed(rhs, inverse[2])
    y3[...] = here
    message[0] = here
    message[1:5] = sums4[pl.ds((1 - x_bit) * 4, 4)]
    for level in range(2):
        for y in range(4):
            y12p[level * 4 + y] = y12[level * 8 + y * 2 + core]


def level4_sums_kernel(coords, own, part1, part2, part3, sums4):
    sums4[...] = (own[...] + part1[...]) + (part2[...] + part3[...])


def level4_pair_kernel(coords, y3, sums4, received, own, message1, message2, message3):
    y_at, x_bit = coords[1], coords[2] & 1
    for j, out in enumerate((own, message1, message2, message3)):
        row = y_at ^ j
        out[0] = y3[...]
        out[1] = received[0]
        out[2] = sums4[x_bit * 4 + row] + received[1 + row]


def level4_pack_kernel(coords, own, part1, part2, part3, r8, low16, total):
    y_at, x_bit = coords[1], coords[2] & 1
    for j, part in enumerate((own, part1, part2, part3)):
        low16[x_bit * 4 + (y_at ^ j)] = part[0]
        low16[(1 - x_bit) * 4 + (y_at ^ j)] = part[1]
    low16[8:16] = r8[...]
    total[...] = (own[2] + part1[2]) + (part2[2] + part3[2])


def level5_sums_kernel(coords, own, part1, part2, part3, sums5):
    sums5[...] = (own[...] + part1[...]) + (part2[...] + part3[...])


def half_lefts(left, core, line, mine, other, rest):
    for p in range(8):
        left[32 + 2 * p + core] = stacked(mine[p])
        left[32 + 2 * p + 1 - core] = stacked(other[p])
    for level in range(2):
        for y in range(4):
            at = level * 16 + line * 8 + 2 * y
            left[at + core] = stacked(mine[8 + level * 4 + y])
            left[at + 1 - core] = stacked(other[8 + level * 4 + y])
        rest(level, level * 16 + (1 - line) * 8)


def own_half_lefts(left, coords, low, other, y12):
    def rest(level, at):
        for m in range(8):
            left[at + m] = stacked(y12[level * 8 + m])

    half_lefts(left, coords[0], 1 - (coords[2] & 1), low, other, rest)


def level4_kernel(
    coords, low, other, y12, total, sums5, inverse, mats, y4, operand, left
):
    own_half_lefts(left, coords, low, other, y12)
    terms = sum_times_transposed([left[m] for m in range(48)], [mats[m] for m in range(48)])
    here = times_transposed(-total[...] - fold(terms), inverse[3])
    y4[...] = here
    for p in range(16):
        operand[p, 0] = here
        operand[p, 1] = sums5[p]


def fetch_half(coupling, half, target, sems):
    copies = []
    for level in range(3):
        source = coupling.at[pl.ds(RUNS[5, 1] + level * 32 + half * 16, 16)]
        copies.append(
            pltpu.make_async_copy(source, target.at[pl.ds(level * 16, 16)], sems.at[level])
        )
        copies[-1].start()
    return copies


def half_products(copies, left, mats):
    total = None
    for level, copy in enumerate(copies):
        copy.wait()
        rows = range(level * 16, level * 16 + 16)
        part = sum_times_transposed([left[m] for m in rows], [mats[m] for m in rows])
        total = part if total is None else total + part
    return total


def level5_own_kernel(coords, low, other, y12, coupling, acc, mats, sems, left):
    copies = fetch_half(coupling, coords[2] >> 1, mats, sems)
    own_half_lefts(left, coords, low, other, y12)
    acc[...] = half_products(copies, left, mats)


def level5_far_kernel(
    coords, low, other, line, line_other, own, coupling, acc, mats54, mats, sems, left, sem
):
    copies = fetch_half(coupling, 1 - (coords[2] >> 1), mats, sems)
    last = pltpu.make_async_copy(coupling.at[pl.ds(RUNS[5, 4], 32)], mats54, sem)
    last.start()
    core = coords[0]

    def rest(level, at):
        for y in range(4):
            left[at + 2 * y + core] = stacked(line[level * 4 + y])
            left[at + 2 * y + 1 - core] = stacked(line_other[level * 4 + y])

    half_lefts(left, core, coords[2] & 1, low, other, rest)
    acc[...] = own[...] + half_products(copies, left, mats)
    last.wait()


def level5_kernel(coords, acc, mine, other, inverse, mats, x5, own, theirs, left, pair):
    core = coords[0]
    total = mine[0, 1]
    for p in range(1, 16):
        total = total + mine[p, 1]
    for p in range(16):
        left[p * 2 + core] = stacked(mine[p, 0])
        left[p * 2 + 1 - core] = stacked(other[p, 0])
    terms = acc[...] + sum_times_transposed(
        [left[m] for m in range(32)], [mats[m] for m in range(32)]
    )
    solved = times_transposed(-total - fold(terms), inverse[4])
    here = times(solved, inverse[4])
    x5[...] = here
    wide = wide_left(here)
    for p in range(16):
        pair[2 * p], pair[2 * p + 1] = two_times(wide, mats[2 * p], mats[2 * p + 1])
    for p in range(16):
        own[p] = pair[2 * p + core]
        theirs[p] = pair[2 * p + 1 - core]


def level4_operand_kernel(coords, x5, own, received, operand):
    for p in range(16):
        operand[p, 0] = own[p] + received[p]
        operand[p, 1] = x5[...]


def level5_back_kernel(coords, x5, coupling, spread, mats4, mats, sems, sem):
    fetch(coupling, RUNS[5, 1], 96, mats, sems)
    last = pltpu.make_async_copy(coupling.at[pl.ds(RUNS[4, 1], 48)], mats4, sem)
    last.start()
    wide = wide_left(x5[...])

    def step(i, _):
        fetched(coupling, RUNS[5, 1], mats, sems, i)
        for k in range(0, CHUNK, 2):
            at = i * CHUNK + k
            spread[at], spread[at + 1] = two_times(wide, mats[at], mats[at + 1])
        return 0

    lax.fori_loop(0, 96 // CHUNK, step, 0)
    last.wait()


def level4_back_kernel(coords, parts, y4, spread, inverse, mats, x4, x5p, mine, theirs, all4):
    core, half = coords[0], coords[2] >> 1
    total = parts[0, 0]
    for p in range(1, 16):
        total = total + parts[p, 0]
    for p in range(16):
        x5p[p] = parts[p, 1]
    here = times(y4[...] - total, inverse[3])
    x4[...] = here
    wide = wide_left(here)
    for level in range(3):
        for pair in range(16):
            mine[pair, level] = spread[level * 32 + pair * 2 + core]
            theirs[pair, level] = spread[level * 32 + pair * 2 + 1 - core]
        for pair in range(8):
            at = level * 16 + pair * 2
            all4[0], all4[1] = two_times(wide, mats[at], mats[at + 1])
            mine[half * 8 + pair, level] += all4[core]
            theirs[half * 8 + pair, level] += all4[1 - core]


def level3_operand_kernel(coords, x4, mine, received, operand):
    for p in range(16):
        operand[p, 0:3] = mine[p] + received[p]
        operand[p, 3] = x4[...]


def level3_back_kernel(coords, parts, y3, inverse, mats, x3, x4p, mine, theirs, spread):
    core, y_at = coords[0], coords[1]
    sums = []
    for level in range(3):
        total = parts[0, level]
        for p in range(1, 16):
            total = total + parts[p, level]
        sums.append(total)
    for p in range(8):
        x4p[p] = parts[(coords[2] >> 1) * 8 + p, 3]
    here = times(y3[...] - sums[2], inverse[2])
    x3[...] = here
    wide = wide_left(here)
    for pair in range(8):
        spread[2 * pair], spread[2 * pair + 1] = two_times(wide, mats[2 * pair], mats[2 * pair + 1])
    for level in range(2):
        spread[level * 8 + y_at * 2 + core] += sums[level]
    for pair in range(8):
        mine[pair] = spread[2 * pair + core]
        theirs[pair] = spread[2 * pair + 1 - core]


def pair_message_kernel(coords, mine, received, x3, keep, message):
    half = coords[1] >> 1
    for level in range(2):
        for out, part in ((keep, half), (message, 1 - half)):
            rows = pl.ds(level * 4 + part * 2, 2)
            out[level * 2 : level * 2 + 2] = mine[rows] + received[rows]
    message[4] = x3[...]


def pair_sum_kernel(coords, keep, received, x3, message):
    message[0:4] = keep[...] + received[0:4]
    message[4] = x3[...]
    message[5] = received[4]


def pair_total_kernel(coords, message, received, out):
    out[0:4] = message[0:4] + received[0:4]
    out[4:6] = message[4:6]
    out[6:8] = received[4:6]


def level12_back_kernel(
    coords, mine, other, solved, own6, core6, y6, diagonal6, own1, own2, x123, terms
):
    core, y_at = coords[0], coords[1]
    y_bit = y_at & 1
    for source, parity in ((mine, core), (other, 1 - core)):
        for level in range(2):
            for y in range(2):
                terms[level * 4 + y * 2 + parity] = source[level * 2 + y]
        for k, dy in enumerate((0, 3, 1, 2)):
            x123[6 + (y_at ^ dy) * 2 + parity] = source[4 + k]
    members = [
        ((y_bit ^ dy) * 2 + (core ^ dc), dy, core ^ dc) for dy in range(2) for dc in range(2)
    ]
    mats = (own6, core6, y6, diagonal6)
    for k, ((index, dy, at), mat) in enumerate(zip(members, mats)):
        here = times(solved[4 + index] - terms[4 + index], mat[1])
        x123[2 + index] = here
        if k == 0:
            own2[...] = here
        wide = wide_left(here)
        for m in range(0, 4, 2):
            first, second = two_times(wide, mat[2 + m], mat[3 + m])
            terms[m] += first
            terms[m + 1] += second
    for k in range(2):
        index, dy, at = members[k]
        here = times(solved[index] - terms[index], mats[k][0])
        x123[at] = here
        if k == 0:
            own1[...] = here


LOW = 14
AT_ONCE = 8


def pack_kernel(coords, part0, part1, part2, part3, out):
    for j, part in enumerate((part0, part1, part2, part3)):
        out[j] = part[...]


def pack(coords, parts):
    return call(pack_kernel, "pack", coords, parts, [(4, *parts[0].shape)])[0]


def place(blocks, index, front, j, value):
    high, low = split(value)
    at = pl.multiple_of((front ^ j) * COLS, COLS)
    blocks[index, pl.ds(at, COLS), :] = high
    blocks[index, pl.ds(BLK + at, COLS), :] = low


def leaf_high_kernel(
    coords, pattern, load, inverse, coupling, x4m, x4o, x5m, x5o,
    rhs, couplings, items,
    loads, inverses, blocks, sems,
):
    count = couplings.shape[0]
    core, front = coords[0], coords[3]
    copies = leaf_copies(load, inverse, coupling, loads, inverses, couplings, sems, count)
    for copy in copies:
        copy.start()

    def note(i, found):
        items[1 + found] = i
        return found + (pattern[i >> 3, i & 7] < LOW).astype(jnp.int32)

    items[0] = lax.fori_loop(0, count * 8, note, jnp.int32(0))
    blocks[48] = jnp.zeros((2 * BLK, BLK), BF16)
    for j in range(4):
        for p in range(8):
            place(blocks, 2 * p + core, front, j, x4m[j, p])
            place(blocks, 2 * p + 1 - core, front, j, x4o[j, p])
        for p in range(16):
            place(blocks, 16 + 2 * p + core, front, j, x5m[j, p])
            place(blocks, 16 + 2 * p + 1 - core, front, j, x5o[j, p])
    copies[0].wait()
    copies[1].wait()
    for k in range(count // PER_COPY):
        copies[2 + k].wait()
        for b in range(k * PER_COPY, (k + 1) * PER_COPY):
            here = times_transposed(loads[:, b * BLK : (b + 1) * BLK], inverses[b])
            total = None
            for q in range(0, 8, 2):
                indices = [pattern[b, q + k2] for k2 in range(2)]
                chosen = [jnp.where(index < LOW, 48, index - LOW) for index in indices]
                left = jnp.concatenate([blocks[c] for c in chosen], axis=1)
                right = jnp.concatenate([beside(couplings[b, q + k2]) for k2 in range(2)], axis=0)
                part = dot_nn(left, right)
                total = part if total is None else total + part
            rhs[b] = here - fold(total)


def leaf_high(coords, pattern, load_leaf, leaf_inverse, leaf_coupling, gathered):
    blocks = leaf_inverse.shape[0]
    vmem = pl.BlockSpec(memory_space=pltpu.VMEM)
    return pl.pallas_call(
        leaf_high_kernel,
        name="leaf_high",
        out_shape=[
            jax.ShapeDtypeStruct((blocks, BLK, BLK), F32),
            jax.ShapeDtypeStruct(leaf_coupling.shape, F32),
            jax.ShapeDtypeStruct((blocks * 8 + 2,), jnp.int32),
        ],
        grid_spec=pltpu.PrefetchScalarGridSpec(
            num_scalar_prefetch=2,
            grid=(1,),
            in_specs=[pl.BlockSpec(memory_space=pltpu.HBM)] * 3 + [vmem] * 4,
            out_specs=[vmem, vmem, pl.BlockSpec(memory_space=pltpu.SMEM)],
            scratch_shapes=[
                pltpu.VMEM(load_leaf.shape, F32),
                pltpu.VMEM(leaf_inverse.shape, F32),
                pltpu.VMEM((49, 2 * BLK, BLK), BF16),
                pltpu.SemaphoreType.DMA((2 + blocks // PER_COPY,)),
            ],
        ),
        compiler_params=pltpu.CompilerParams(vmem_limit_bytes=VMEM_BYTES),
        cost_estimate=cost(8),
    )(coords, pattern, load_leaf, leaf_inverse, leaf_coupling, *gathered)


def leaf_low_kernel(
    coords, pattern, items, low0, low1, low2, low3, rhs, inverse, couplings,
    out,
    blocks, acc, solved, sems,
):
    front, count = coords[3], items[0]
    acc[...] = rhs[...]
    blocks[LOW] = jnp.zeros((2 * BLK, BLK), BF16)
    for j, low in enumerate((low0, low1, low2, low3)):
        for a in range(LOW):
            place(blocks, a, front, j, low[a])

    def step(t, _):
        for k in range(AT_ONCE):
            at = t * AT_ONCE + k
            item = jnp.where(at < count, items[1 + jnp.minimum(at, count)], 0)
            index = jnp.where(at < count, pattern[item >> 3, item & 7], LOW)
            right = beside(couplings[item >> 3, item & 7])
            acc[item >> 3] -= fold(dot_nn(blocks[index], right))
        return 0

    lax.fori_loop(0, (count + AT_ONCE - 1) // AT_ONCE, step, 0)
    copies = []
    for b in range(rhs.shape[0]):
        solved[b] = times(acc[b], inverse[b])
        copies.append(
            pltpu.make_async_copy(solved.at[b], out.at[:, b * BLK : (b + 1) * BLK], sems.at[b])
        )
        copies[-1].start()
    for copy in copies:
        copy.wait()


def leaf_low(coords, pattern, items, lows, rhs, leaf_inverse, couplings):
    blocks = leaf_inverse.shape[0]
    vmem = pl.BlockSpec(memory_space=pltpu.VMEM)
    return pl.pallas_call(
        leaf_low_kernel,
        name="leaf_low",
        out_shape=jax.ShapeDtypeStruct((BLK, blocks * BLK), F32),
        grid_spec=pltpu.PrefetchScalarGridSpec(
            num_scalar_prefetch=3,
            grid=(1,),
            in_specs=[vmem] * 7,
            out_specs=pl.BlockSpec(memory_space=pltpu.HBM),
            scratch_shapes=[
                pltpu.VMEM((LOW + 1, 2 * BLK, BLK), BF16),
                pltpu.VMEM((blocks, BLK, BLK), F32),
                pltpu.VMEM((blocks, BLK, BLK), F32),
                pltpu.SemaphoreType.DMA((blocks,)),
            ],
        ),
        compiler_params=pltpu.CompilerParams(vmem_limit_bytes=VMEM_BYTES),
        cost_estimate=cost(4),
    )(coords, pattern, items, *lows, rhs, leaf_inverse, couplings)


def across(value, mask):
    return lax.ppermute(value, "leaf", [(i, i ^ mask) for i in range(32)])


def across_front(value, mask):
    return lax.ppermute(value, "front", [(i, i ^ mask) for i in range(4)])


def swap16(value):
    groups = [[c + 2 * p for p in range(16)] for c in (0, 1)]
    return lax.all_to_all(value, "leaf", 0, 0, axis_index_groups=groups)


def local(
    load_leaf, leaf_inverse, leaf_coupling, leaf_pattern, load_sep, sep_inverse, sep_coupling
):
    leaf_at = lax.axis_index("leaf")
    coords = jnp.stack([leaf_at & 1, (leaf_at >> 1) & 3, leaf_at >> 3, lax.axis_index("front")])
    coords = coords.astype(jnp.int32)
    pattern = leaf_pattern
    one = (COLS, BLK)
    wide = (2 * COLS, 2 * BLK)
    left = lambda count: pltpu.VMEM((count, 2 * COLS, BLK), BF16)
    own6 = jnp.concatenate([sep_inverse[0:2], sep_coupling[0:4]], axis=0)
    mine13, theirs13, mine45, theirs45 = leaf_forward(
        coords, pattern, load_leaf, leaf_inverse, leaf_coupling, load_sep
    )
    *parts13, theirs45, own6 = front_parts(
        coords, mine13, across(theirs13, 1), (0, 10), through=[theirs45, own6]
    )
    parts13 = [parts13[0]] + [across_front(parts13[j], j) for j in (1, 2, 3)]
    y6 = across(own6, 2)
    core6 = across(own6, 1)
    parts45 = front_parts(coords, mine45, across(theirs45, 1), (0, 8, 24))
    parts4, parts5 = parts45[0:4], parts45[4:8]
    inverses, mats3, mats4 = preload(
        coords,
        [(sep_inverse, 0, 5), (sep_coupling, RUNS[3, 1], 16), (sep_coupling, RUNS[4, 1], 48)],
        after=[parts45[0]],
    )
    keep, message, y6 = call(
        level12_message_kernel,
        "level12_message",
        coords,
        parts13,
        [(8, *one), (8, *one)],
        after=[parts45[0], mats3],
        through=[y6],
    )
    diagonal6 = across(y6, 1)
    group = [own6, core6, y6, diagonal6]
    parts4 = [parts4[0]] + [across_front(parts4[j], j) for j in (1, 2, 3)]
    solved12, message = call(
        level12_kernel,
        "level12",
        coords,
        [keep, across(message, 2), *group],
        [(9, *one), (9, *one)],
        us=2,
        scratch=[left(4), pltpu.VMEM((8, 128), F32)],
    )
    (sums4,) = call(
        level4_sums_kernel, "level4_sums", coords, parts4, [(8, *one)]
    )
    parts5 = [parts5[0]] + [across_front(parts5[j], j) for j in (1, 2, 3)]
    y3, message, y12, y12p = call(
        level3_kernel,
        "level3",
        coords,
        [solved12, across(message, 6), sums4, inverses, mats3],
        [one, (5, *one), (16, *one), (8, *one)],
        us=2,
        scratch=[left(16)],
    )
    (sums5,) = call(level5_sums_kernel, "level5_sums", coords, parts5, [(16, *one)])
    r8 = across(y12p, 8)
    own, *messages = call(
        level4_pair_kernel,
        "level4_pair",
        coords,
        [y3, sums4, across(message, 8)],
        [(3, *one)] * 4,
    )
    parts = [own] + [across(messages[j - 1], 2 * j) for j in (1, 2, 3)]
    low16, total4 = call(
        level4_pack_kernel,
        "level4_pack",
        coords,
        [*parts, r8],
        [(16, *one), one],
        after=[sums5],
    )
    other16 = across(low16, 1)
    far16 = across(low16, 24)
    line8 = across(y12p, 24)
    line_other8 = across(line8, 1)
    y4, operand = call(
        level4_kernel,
        "level4",
        coords,
        [low16, other16, y12, total4, sums5, inverses, mats4],
        [one, (16, 2, *one)],
        us=3,
        scratch=[left(48)],
    )
    y4m = swap16(operand)
    far_other16 = across(far16, 1)
    (own5,) = call(
        level5_own_kernel,
        "level5_own",
        coords,
        [low16, other16, y12, sep_coupling],
        [wide],
        us=4,
        in_hbm=(3,),
        scratch=[pltpu.VMEM((48, BLK, BLK), F32), pltpu.SemaphoreType.DMA((3,)), left(48)],
        limit=LARGE_VMEM_BYTES,
    )
    acc5, mats54 = call(
        level5_far_kernel,
        "level5_far",
        coords,
        [far16, far_other16, line8, line_other8, own5, sep_coupling],
        [wide, (32, BLK, BLK)],
        us=4,
        in_hbm=(5,),
        scratch=[
            pltpu.VMEM((48, BLK, BLK), F32),
            pltpu.SemaphoreType.DMA((3,)),
            left(48),
            pltpu.SemaphoreType.DMA,
        ],
        limit=LARGE_VMEM_BYTES,
    )
    y4m, acc5, mats54 = lax.optimization_barrier((y4m, acc5, mats54))
    y4o = across(y4m, 1)
    x5, own4, theirs4 = call(
        level5_kernel,
        "level5",
        coords,
        [acc5, y4m, y4o, inverses, mats54],
        [one, (16, *one), (16, *one)],
        us=4,
        scratch=[left(32), pltpu.VMEM((32, *one), F32)],
    )
    (operand,) = call(
        level4_operand_kernel,
        "level4_operand",
        coords,
        [x5, own4, across(theirs4, 1)],
        [(16, 2, *one)],
    )
    sums4 = swap16(operand)
    spread, mats4 = call(
        level5_back_kernel,
        "level5_back",
        coords,
        [x5, sep_coupling],
        [(96, *one), (48, BLK, BLK)],
        us=6,
        in_hbm=(1,),
        scratch=[*matrices(96), pltpu.SemaphoreType.DMA],
        limit=LARGE_VMEM_BYTES,
    )
    x4, x5p, mine, theirs = call(
        level4_back_kernel,
        "level4_back",
        coords,
        [sums4, y4, spread, inverses, mats4],
        [one, (16, *one), (16, 3, *one), (16, 3, *one)],
        us=2,
        scratch=[pltpu.VMEM((2, *one), F32)],
    )
    x5s = [x5p] + [across_front(x5p, j) for j in (1, 2, 3)]
    (operand,) = call(
        level3_operand_kernel,
        "level3_operand",
        coords,
        [x4, mine, across(theirs, 1)],
        [(16, 4, *one)],
    )
    parts3 = swap16(operand)
    x3, x4p, mine, theirs = call(
        level3_back_kernel,
        "level3_back",
        coords,
        [parts3, y3, inverses, mats3],
        [one, (8, *one), (8, *one), (8, *one)],
        us=1.5,
        scratch=[pltpu.VMEM((16, *one), F32)],
    )
    x5m = pack(coords, x5s)
    x5o = across(x5m, 1)
    x4s = [x4p] + [across_front(x4p, j) for j in (1, 2, 3)]
    keep, message = call(
        pair_message_kernel,
        "pair_message",
        coords,
        [mine, across(theirs, 1), x3],
        [(4, *one), (5, *one)],
        after=x5s[1:],
    )
    (message,) = call(
        pair_sum_kernel, "pair_sum", coords, [keep, across(message, 6), x3], [(6, *one)]
    )
    (mine,) = call(
        pair_total_kernel,
        "pair_total",
        coords,
        [message, across(message, 2)],
        [(8, *one)],
        after=x4s[1:],
    )
    x1, x2, x123 = call(
        level12_back_kernel,
        "level12_back",
        coords,
        [mine, across(mine, 1), solved12, *group],
        [one, one, (14, *one)],
        us=2,
        scratch=[pltpu.VMEM((8, *one), F32)],
    )
    x4m = pack(coords, x4s)
    x4o = across(x4m, 1)
    rhs, couplings, items = leaf_high(
        coords, pattern, load_leaf, leaf_inverse, leaf_coupling, [x4m, x4o, x5m, x5o]
    )
    lows = [x123] + [across_front(x123, j) for j in (1, 2, 3)]
    solution_leaf = leaf_low(coords, pattern, items, lows, rhs, leaf_inverse, couplings)
    solution_sep = jnp.concatenate([x1, x2, x3, x4, x5], axis=1)
    return solution_leaf, solution_sep


def solution(mesh):
    return jax.shard_map(
        local,
        mesh=mesh,
        in_specs=(
            P(None, ("leaf", "front")),
            P(("leaf", "front"), None, None),
            P(("leaf", "front"), None, None, None),
            P(("leaf", "front"), None),
            P("front", "leaf"),
            P("leaf", None, None),
            P("leaf", None, None),
        ),
        out_specs=(P(None, ("leaf", "front")), P("front", "leaf")),
        check_vma=False,
    )
```
